128 devices in a mesh: row: 16 (over z, y_hi, core), loop: 8 (over x, y_lo).
Axes of the slice: x: 4, y: 4 (y_hi: 2, y_lo: 2; y = y_hi * 2 + y_lo), z: 4, core: 2. Of those that a mesh axis runs over, the one named last changes fastest.
Arguments:
- student_image: bfloat16 [20480, 1024], P(('row', 'loop')), may hold values from -12 to 12
- student_text: bfloat16 [20480, 1024], P(('row', 'loop')), may hold values from -12 to 12
- teacher_image: bfloat16 [20480, 1024], P('row', 'loop'), may hold values from -12 to 12
- teacher_text: bfloat16 [20480, 1024], P('row', 'loop'), may hold values from -12 to 12
- student_scale: float32 [1], replicated, may hold values from 30 to 100
- teacher_scale: float32 [1], replicated, may hold values from 30 to 100
Outputs:
- loss: float32 [1], replicated
- grad_image: bfloat16 [20480, 1024], P(('row', 'loop'))
- grad_text: bfloat16 [20480, 1024], P(('row', 'loop'))
The draws below stay inside these ranges and needn't reach their ends.
All inputs are finite; a program needn't handle non-finite values.
Results may differ from the reference program's by a relative error of at most 0.014.
The reference program's roundings to bfloat16 on the way (of `simg` and `grad_logits`) count: a program that leaves them out, or rounds other values in their place, can miss the bound.
Values may be sent and summed in bfloat16 or wider, within the bound.
No kernel may reach another device: no remote copies, remote signals or barrier semaphores. Data moves between devices by JAX's collectives and lax.ppermute only.
A program may use at most 128 MiB of HBM per device.

```python
import math
import jax
import jax.numpy as jnp
from jax import lax

CODE = 1024
ROWS_DEV = 160
BATCH = 20480
ROW_BLOCK = 1280
N_ROW = 16
N_LOOP = 8


def raw_codes(key, stream):
    base_key = jax.random.fold_in(key, stream)
    first = jax.random.normal(jax.random.fold_in(base_key, 1), (BATCH, CODE), jnp.float32)
    second = jax.random.normal(jax.random.fold_in(base_key, 2), (BATCH, CODE), jnp.float32)
    return (first, second)


def blend_weights():
    groups = BATCH // ROW_BLOCK
    group = (jnp.arange(BATCH, dtype=jnp.int32) // ROW_BLOCK).astype(jnp.float32)
    frac = group / float(max(groups - 1, 1))
    theta = 0.1 + (0.5 * math.pi - 0.1) * frac
    return (jnp.cos(theta)[:, None], jnp.sin(theta)[:, None])


def pair_codes(key, stream):
    teach_img, teach_txt = raw_codes(key, 202)
    if stream == 202:
        images, text_rows = (teach_img, teach_txt)
    else:
        own_img, own_txt = raw_codes(key, 101)
        near, far = blend_weights()
        images = near * teach_img + far * own_img
        text_rows = near * teach_txt + far * own_txt
    return (jnp.clip(images, -6.0, 6.0), jnp.clip(text_rows, -6.0, 6.0))


def logit_scales(key):
    scale_key = jax.random.fold_in(key, 300)
    student = jnp.exp(jax.random.uniform(jax.random.fold_in(scale_key, 1), (1,), jnp.float32, math.log(30.0), math.log(100.0)))
    factor = jnp.exp(jax.random.uniform(jax.random.fold_in(scale_key, 2), (1,), jnp.float32, -0.1, 0.1))
    teacher = jnp.clip(student * factor, 30.0, 100.0)
    return (student, teacher)


def draw_student_image(key, part):
    return pair_codes(key, 101)[0].astype(jnp.bfloat16)


def draw_student_text(key, part):
    return pair_codes(key, 101)[1].astype(jnp.bfloat16)


def draw_teacher_image(key, part):
    return pair_codes(key, 202)[0].astype(jnp.bfloat16)


def draw_teacher_text(key, part):
    return pair_codes(key, 202)[1].astype(jnp.bfloat16)


def draw_student_scale(key, part):
    return logit_scales(key)[0]


def draw_teacher_scale(key, part):
    return logit_scales(key)[1]


def setup_inputs(seed: int = 0) -> dict:
    key_of = jax.random.split(jax.random.key(seed), 7)
    student_image = draw_student_image(jax.random.fold_in(key_of[6], 71), 0)
    student_text = draw_student_text(jax.random.fold_in(key_of[6], 71), 0)
    teacher_image = draw_teacher_image(jax.random.fold_in(key_of[6], 71), 0)
    teacher_text = draw_teacher_text(jax.random.fold_in(key_of[6], 71), 0)
    student_scale = draw_student_scale(jax.random.fold_in(key_of[6], 71), 0)
    teacher_scale = draw_teacher_scale(jax.random.fold_in(key_of[6], 71), 0)
    return dict(student_image=student_image, student_text=student_text, teacher_image=teacher_image, teacher_text=teacher_text, student_scale=student_scale, teacher_scale=teacher_scale)


EPS = 1e-06

def unit_rows(codes):
    values = codes.astype(jnp.float32)
    norms = jnp.sqrt(lax.optimization_barrier(jnp.sum(values * values, axis=1, keepdims=True)) + EPS)
    return (values / norms, norms)

def back_norm(grad_unit, units, norms):
    inner = lax.optimization_barrier(jnp.sum(grad_unit * units, axis=1, keepdims=True))
    return ((grad_unit - units * inner) / norms).astype(jnp.bfloat16)

def rounded_term(term):
    narrow = lax.optimization_barrier(term.astype(jnp.bfloat16))
    return narrow.astype(jnp.float32)

def reference(student_image, student_text, teacher_image, teacher_text, student_scale, teacher_scale):
    simg_unit, simg_norm = unit_rows(student_image)
    stxt_unit, stxt_norm = unit_rows(student_text)
    simg = simg_unit.astype(jnp.bfloat16)
    stxt = stxt_unit.astype(jnp.bfloat16)
    timg = unit_rows(teacher_image)[0].astype(jnp.bfloat16)
    ttxt = unit_rows(teacher_text)[0].astype(jnp.bfloat16)
    sscale = student_scale[0]
    tscale = teacher_scale[0]
    block = ROWS_DEV * N_LOOP
    count = BATCH // block
    stxt_split = stxt.reshape(N_ROW, N_LOOP, ROWS_DEV, CODE)

    def one_block(carry, index):
        total, text_acc = carry
        start = (index * block).astype(jnp.int32)
        simg_b = lax.dynamic_slice_in_dim(simg, start, block, 0)
        timg_b = lax.dynamic_slice_in_dim(timg, start, block, 0)
        slog = sscale * jnp.dot(simg_b, stxt.T, preferred_element_type=jnp.float32)
        tlog = tscale * jnp.dot(timg_b, ttxt.T, preferred_element_type=jnp.float32)
        lses = jax.nn.logsumexp(slog, axis=1)
        lset = jax.nn.logsumexp(tlog, axis=1)
        probt = jnp.exp(tlog - lset[:, None])
        probs = jnp.exp(slog - lses[:, None])
        diverge = lax.optimization_barrier(jnp.sum(probt * (tlog - slog), axis=1)) - lset + lses
        grad_logits = (sscale * (probs - probt)).astype(jnp.bfloat16)
        grad_split = grad_logits.reshape(block, N_ROW, N_LOOP, ROWS_DEV)
        dimg = jnp.zeros((block, CODE), jnp.float32)
        for column_class in range(N_LOOP):
            class_cols = grad_split[:, :, column_class, :].reshape(block, N_ROW * ROWS_DEV)
            class_text = stxt_split[:, column_class, :, :].reshape(N_ROW * ROWS_DEV, CODE)
            dimg = dimg + rounded_term(jnp.dot(class_cols, class_text, preferred_element_type=jnp.float32))
        text_term = jnp.dot(grad_logits.T, simg_b, preferred_element_type=jnp.float32)
        text_acc = text_acc + rounded_term(text_term)
        return ((total + jnp.sum(diverge), text_acc), dimg)
    start_carry = (jnp.zeros((), jnp.float32), jnp.zeros((BATCH, CODE), jnp.float32))
    (total, dtxt), dimg_blocks = lax.scan(one_block, start_carry, jnp.arange(count, dtype=jnp.int32))
    dimg = dimg_blocks.reshape(BATCH, CODE)
    loss = (total / BATCH).reshape(1)
    return (loss, back_norm(dimg, simg_unit, simg_norm), back_norm(dtxt, stxt_unit, stxt_norm))
```

```python
import jax
import jax.numpy as jnp
from jax import lax
from jax.sharding import PartitionSpec as P

EPS = 1e-06
AXES = ("row", "loop")
SIZES = {"z": 4, "yh": 2, "core": 2, "x": 4, "yl": 2}


def index_of(pos):
    index = 0
    for name, size in SIZES.items():
        index = index * size + pos[name] % size
    return index


def positions():
    found = [{}]
    for name, size in SIZES.items():
        found = [{**pos, name: i} for pos in found for i in range(size)]
    return found


def send(value, **step):
    perm = []
    for pos in positions():
        to = dict(pos)
        for name, by in step.items():
            to[name] = pos[name] + by
        perm.append((index_of(pos), index_of(to)))
    return lax.ppermute(value, AXES, perm=perm)


def swap_bit(value, axis, bit):
    perm = []
    for pos in positions():
        perm.append((index_of(pos), index_of({**pos, axis: pos[axis] ^ bit})))
    return lax.ppermute(value, AXES, perm=perm)


def unit_rows(codes):
    values = codes.astype(jnp.float32)
    norms = jnp.sqrt(jnp.sum(values * values, axis=1, keepdims=True) + EPS)
    return (values / norms, norms)


def back_norm(grad_unit, units, norms):
    inner = jnp.sum(grad_unit * units, axis=1, keepdims=True)
    return ((grad_unit - units * inner) / norms).astype(jnp.bfloat16)


def gather_ring(own, ring, pair, rows_axis=0, pair_axis=0):
    other = send(own, **{pair: 1})
    block = jnp.concatenate([own, other], pair_axis)
    before = send(block, **{ring: 1})
    after = send(block, **{ring: -1})
    half = block.shape[0] // 2
    first = send(before[:half], **{ring: 1})
    second = send(after[half:], **{ring: -1})
    return block, after, first, second, before


def scatter_ring(parts, ring, pair):
    f32 = jnp.float32
    low = lambda v: v.astype(jnp.bfloat16)
    to_next = send(parts[2][0], **{ring: 1})
    to_prev = send(parts[2][1], **{ring: -1})
    ahead = jnp.concatenate([low(parts[1][0].astype(f32) + to_next), parts[1][1]], 0)
    behind = jnp.concatenate([parts[3][0], low(parts[3][1].astype(f32) + to_prev)], 0)
    got = send(ahead, **{ring: 1}).astype(f32) + send(behind, **{ring: -1}).astype(f32)
    rows = parts[0][0].shape[0]
    away = low(parts[0][1].astype(f32) + got[rows:])
    return parts[0][0].astype(f32) + got[:rows] + send(away, **{pair: 1}).astype(f32)


def on_device(
    student_image, student_text, teacher_image, teacher_text, student_scale, teacher_scale
):
    rows = student_image.shape[0]
    loop = lax.axis_index("loop")
    x, yl = loop // 2, loop % 2
    order = jnp.stack([((x + k) % 4) * 2 + (yl ^ j) for k in range(4) for j in range(2)])

    simg_unit, simg_norm = unit_rows(student_image)
    stxt_unit, stxt_norm = unit_rows(student_text)
    simg_own = simg_unit.astype(jnp.bfloat16)
    stxt_own = stxt_unit.astype(jnp.bfloat16)

    simg = jnp.concatenate(gather_ring(simg_own, "x", "yl"), 0)
    mine = jnp.concatenate(gather_ring(stxt_own, "z", "yh"), 0)
    stxt = jnp.concatenate([mine, send(mine, core=1)], 0)

    chunk = teacher_image.shape[1]
    tblock, tafter, tfirst, tsecond, tbefore = gather_ring(teacher_image, "x", "yl", 0, 1)
    tfull = jnp.concatenate(
        [tblock, tafter, jnp.concatenate([tfirst, tsecond], 0), tbefore], 1
    )
    tfull = jnp.take(tfull.reshape(8, rows, -1), order, axis=0).reshape(8 * rows, -1)
    timg = unit_rows(tfull)[0].astype(jnp.bfloat16)

    tt = jnp.take(teacher_text.reshape(8, rows, chunk), order, axis=0).reshape(4, 2, rows, chunk)
    got = send(tt[:, 1], yl=1)
    pairs = jnp.concatenate([tt[:, 0], got], 2)
    ttxt_full = jnp.concatenate(
        [pairs[0], send(pairs[3], x=-1), send(pairs[2], x=2), send(pairs[1], x=1)], 1
    )
    ttxt_own = unit_rows(ttxt_full)[0].astype(jnp.bfloat16)
    mine = jnp.concatenate(gather_ring(ttxt_own, "z", "yh"), 0)
    ttxt = jnp.concatenate([mine, send(mine, core=1)], 0)

    sscale = student_scale[0]
    tscale = teacher_scale[0]
    slog = sscale * jnp.einsum("re,ce->rc", simg, stxt, preferred_element_type=jnp.float32)
    tlog = tscale * jnp.einsum("re,ce->rc", timg, ttxt, preferred_element_type=jnp.float32)
    smax = jnp.max(slog, axis=1)
    tmax = jnp.max(tlog, axis=1)
    sexp = jnp.exp(slog - smax[:, None])
    texp = jnp.exp(tlog - tmax[:, None])
    stats = jnp.stack(
        [smax, tmax, jnp.sum(sexp, axis=1), jnp.sum(texp, axis=1), jnp.sum(texp * (tlog - slog), axis=1)]
    )

    def merge(a, b):
        sm, tm = jnp.maximum(a[0], b[0]), jnp.maximum(a[1], b[1])
        sa, sb = jnp.exp(a[0] - sm), jnp.exp(b[0] - sm)
        ta, tb = jnp.exp(a[1] - tm), jnp.exp(b[1] - tm)
        return jnp.stack(
            [sm, tm, a[2] * sa + b[2] * sb, a[3] * ta + b[3] * tb, a[4] * ta + b[4] * tb]
        )

    def turned(stat, d, e):
        grid = stat.reshape(5, 4, 2, rows)
        grid = jnp.roll(grid, d, axis=1)
        if e:
            grid = grid[:, :, ::-1]
        return grid.reshape(5, 8 * rows)

    stats = merge(stats, turned(send(stats, yl=1), 0, 1))
    near = send(stats, x=-1)
    far = send(stats, x=2)
    back = send(stats, x=1)
    stats = merge(
        merge(stats, turned(far, 2, 0)), merge(turned(near, 1, 0), turned(back, 3, 0))
    )
    smax, tmax, ssum, tsum, cross = stats
    lses = smax + jnp.log(ssum)
    lset = tmax + jnp.log(tsum)
    diverge = cross / tsum - lset + lses
    total = jnp.broadcast_to(jnp.sum(diverge[:rows]), (8, 128))
    for axis, bit in (("yl", 1), ("core", 1), ("x", 1), ("x", 2), ("z", 1), ("z", 2), ("yh", 1)):
        total = total + swap_bit(total, axis, bit)
    loss = (total[0, 0] / (rows * 128)).reshape(1)

    probs = jnp.exp(slog - lses[:, None])
    probt = jnp.exp(tlog - lset[:, None])
    grad_logits = (sscale * (probs - probt)).astype(jnp.bfloat16)

    dtxt = jnp.einsum(
        "rc,re->ce", grad_logits, simg, preferred_element_type=jnp.float32
    ).astype(jnp.bfloat16)
    half = dtxt.shape[0] // 2
    other = send(dtxt[half:], core=1)
    dtxt = (dtxt[:half].astype(jnp.float32) + other).astype(jnp.bfloat16)
    dtxt = scatter_ring(dtxt.reshape(4, 2, rows, -1), "z", "yh")

    dimg = jnp.dot(grad_logits, stxt, preferred_element_type=jnp.float32).astype(jnp.bfloat16)
    dimg = scatter_ring(dimg.reshape(4, 2, rows, -1), "x", "yl")
    return (loss, back_norm(dimg, simg_unit, simg_norm), back_norm(dtxt, stxt_unit, stxt_norm))


def solution(mesh):
    return jax.shard_map(
        on_device,
        mesh=mesh,
        in_specs=(
            P(("row", "loop"), None),
            P(("row", "loop"), None),
            P("row", "loop"),
            P("row", "loop"),
            P(),
            P(),
        ),
        out_specs=(P(), P(("row", "loop"), None), P(("row", "loop"), None)),
        check_vma=False,
    )
```

```python
import functools
import math

import jax
import jax.numpy as jnp
from jax import lax
from jax.experimental import pallas as pl
from jax.experimental.pallas import tpu as pltpu
from jax.sharding import PartitionSpec as P

EPS = 1e-06
AXES = ("row", "loop")
SIZES = {"z": 4, "yh": 2, "core": 2, "x": 4, "yl": 2}
F32, BF16 = jnp.float32, jnp.bfloat16
LOG2E = math.log2(math.e)
LN2 = math.log(2.0)
LANES = 128
VMEM_LIMIT = 60 * 2**20
PAIRS = [(k, j) for k in range(4) for j in range(2)]
VMEM = pl.BlockSpec(memory_space=pltpu.VMEM)
SMEM = pl.BlockSpec(memory_space=pltpu.SMEM)
ANY = pl.BlockSpec(memory_space=pl.ANY)


def index_of(pos):
    index = 0
    for name, size in SIZES.items():
        index = index * size + pos[name] % size
    return index


def positions():
    found = [{}]
    for name, size in SIZES.items():
        found = [{**pos, name: i} for pos in found for i in range(size)]
    return found


def send(value, **step):
    perm = []
    for pos in positions():
        to = dict(pos)
        for name, by in step.items():
            to[name] = pos[name] + by
        perm.append((index_of(pos), index_of(to)))
    return lax.ppermute(value, AXES, perm=perm)


def params(**kw):
    return pltpu.CompilerParams(vmem_limit_bytes=VMEM_LIMIT, **kw)


def shape(dims, dtype):
    return jax.ShapeDtypeStruct(dims, dtype)


def norm_of(values):
    return jnp.sqrt(jnp.sum(values * values, axis=1, keepdims=True) + EPS)


def unit(codes):
    values = codes.astype(F32)
    return (values / norm_of(values)).astype(BF16)


def place(where_ref, k, j):
    return lax.rem(where_ref[0] + k, 4) * 2 + lax.rem(where_ref[1] + j, 2)


def own_kernel(si, ti, image):
    rows = si.shape[0]
    image[:rows, :] = unit(si[...])
    width = ti.shape[1]
    for l in range(8):
        image[rows:, l * width : (l + 1) * width] = ti[l * rows : (l + 1) * rows, :]


def own_image(si, ti):
    rows, code = si.shape
    return pl.pallas_call(
        own_kernel,
        out_shape=shape((2 * rows, code), BF16),
        in_specs=[VMEM] * 2,
        out_specs=VMEM,
        compiler_params=params(),
        name="own_image",
    )(si, ti)


def own_text_kernel(where, st, parts, text):
    rows = st.shape[0]
    text[:rows, :] = unit(st[...])
    values = jnp.concatenate([parts[place(where, k, j)] for k, j in PAIRS], axis=1)
    text[rows:, :] = unit(values)


def own_text(where, st, parts):
    rows, code = st.shape
    return pl.pallas_call(
        own_text_kernel,
        out_shape=shape((2 * rows, code), BF16),
        in_specs=[SMEM, VMEM, VMEM],
        out_specs=VMEM,
        compiler_params=params(),
        name="own_text",
    )(where, st, parts)


def tie(values, after):
    return lax.optimization_barrier((values, after))[0]


def ring_own(own, ring, pair):
    return send(own, **{ring: 1}), send(own, **{ring: -1}), send(own, **{pair: 1})


def ring_other(other, ring):
    return send(other, **{ring: 1}), send(other, **{ring: -1})


def ring_far(before, after_other, ring):
    return send(before, **{ring: 1}), send(after_other, **{ring: -1})


def in_order(own, first, second, third):
    before, after, other = first
    before_other, after_other = second
    far, far_other = third
    return [own, other, after, after_other, far, far_other, before, before_other]


def sum_of(refs):
    return sum(ref[...].astype(F32) for ref in refs)


def block_of(term, blocks, index):
    rows, code = term.shape
    return pl.BlockSpec((rows // blocks, code), lambda i: (index, 0))


def far_sum_kernel(n, *refs):
    two, two_other = refs[2 * n :]
    two[...] = sum_of(refs[:n]).astype(BF16)
    two_other[...] = sum_of(refs[n : 2 * n]).astype(BF16)


def far_sum(terms):
    n = len(terms)
    rows, code = terms[0].shape
    out = pl.BlockSpec((rows // 8, code), lambda i: (0, 0))
    return pl.pallas_call(
        functools.partial(far_sum_kernel, n),
        grid=(1,),
        out_shape=(shape((rows // 8, code), BF16),) * 2,
        in_specs=[block_of(t, 8, 4) for t in terms] + [block_of(t, 8, 5) for t in terms],
        out_specs=(out,) * 2,
        compiler_params=params(),
        name="far_sum",
    )(*terms, *terms)


def ring_add_kernel(n, *refs):
    to_next, to_prev, ahead, behind = refs[2 * n :]
    rows = to_next.shape[0]
    one = sum_of(refs[:n])
    three = sum_of(refs[n : 2 * n])
    ahead[:rows, :] = (one[:rows] + to_next[...].astype(F32)).astype(BF16)
    ahead[rows:, :] = one[rows:].astype(BF16)
    behind[:rows, :] = three[:rows].astype(BF16)
    behind[rows:, :] = (three[rows:] + to_prev[...].astype(F32)).astype(BF16)


def ring_add(terms, to_next, to_prev):
    n = len(terms)
    rows, code = to_next.shape
    half = pl.BlockSpec((rows, code), lambda i: (0, 0))
    out = pl.BlockSpec((2 * rows, code), lambda i: (0, 0))
    return pl.pallas_call(
        functools.partial(ring_add_kernel, n),
        grid=(1,),
        out_shape=(shape((2 * rows, code), BF16),) * 2,
        in_specs=[block_of(t, 4, 1) for t in terms]
        + [block_of(t, 4, 3) for t in terms]
        + [half, half],
        out_specs=(out,) * 2,
        compiler_params=params(),
        name="ring_add",
    )(*terms, *terms, to_next, to_prev)


def pair_sum_kernel(*refs):
    refs[-1][...] = sum_of(refs[:-1]).astype(BF16)


def pair_sum(terms, near):
    rows, code = near[0].shape
    return pl.pallas_call(
        pair_sum_kernel,
        grid=(1,),
        out_shape=shape((rows // 2, code), BF16),
        in_specs=[block_of(t, 8, 1) for t in terms] + [block_of(t, 2, 1) for t in near],
        out_specs=pl.BlockSpec((rows // 2, code), lambda i: (0, 0)),
        compiler_params=params(),
        name="pair_sum",
    )(*terms, *near)


def final_kernel(*refs):
    codes, out = refs[-2:]
    total = sum_of(refs[:-2])
    values = codes[...].astype(F32)
    norm = norm_of(values)
    units = values / norm
    inner = jnp.sum(total * units, axis=1, keepdims=True)
    out[...] = ((total - units * inner) / norm).astype(BF16)


def finish(terms, near, got, codes):
    own = pl.BlockSpec(codes.shape, lambda i: (0, 0))
    return pl.pallas_call(
        final_kernel,
        grid=(1,),
        out_shape=shape(codes.shape, BF16),
        in_specs=[own] * (len(terms) + len(near) + 2),
        out_specs=own,
        compiler_params=params(),
        name="finish",
    )(*terms, *near, got, codes)


def fetch_images(where, images, held, sem, rows):
    copies = []
    for n, (k, j) in enumerate(PAIRS):
        start = pl.multiple_of(place(where, k, j) * rows, rows)
        copies.append(
            pltpu.make_async_copy(
                images[n].at[pl.ds(0, rows), :], held.at[pl.ds(start, rows), :], sem.at[n]
            )
        )
    return copies


def fetch_texts(texts, held, sem, rows, part):
    return [
        pltpu.make_async_copy(
            texts[n].at[pl.ds(part * rows, rows), :], held.at[pl.ds(n * rows, rows), :], sem.at[n]
        )
        for n in range(16)
    ]


def wait_texts(copies, step, columns, rows):
    done = 0
    for at in range(16 * rows // columns):
        need = min(16, -(-(at + 1) * columns // rows))

        @pl.when(step == at)
        def _():
            for copy in copies[done:need]:
                copy.wait()

        done = need


ROW_TILE = 256
COLS = 512


def lanes_of(value):
    return [value[:, n * LANES : (n + 1) * LANES] for n in range(value.shape[1] // LANES)]


def student_kernel(where, scale, *refs):
    images, texts = refs[:8], refs[8:24]
    slog, mout, sout = refs[24:27]
    held, text, sem_image, sem_text = refs[27:]
    step = pl.program_id(0)
    rows = held.shape[0] // 8

    text_copies = fetch_texts(texts, text, sem_text, rows, 0)

    @pl.when(step == 0)
    def _():
        image_copies = fetch_images(where, images, held, sem_image, rows)
        for copy in image_copies + text_copies:
            copy.start()
        for copy in image_copies:
            copy.wait()
        mout[...] = jnp.full(mout.shape, -1e30, F32)
        sout[...] = jnp.zeros(sout.shape, F32)

    wait_texts(text_copies, step, COLS, rows)
    factor = scale[0] * LOG2E
    cols = text[pl.ds(pl.multiple_of(step * COLS, COLS), COLS), :]

    for r in range(held.shape[0] // ROW_TILE):
        at = pl.ds(r * ROW_TILE, ROW_TILE)
        s = factor * lax.dot_general(
            held[at, :], cols, (((1,), (1,)), ((), ())), preferred_element_type=F32
        )
        slog[at, :] = s
        old = mout[at, :]
        parts = lanes_of(s)
        top = functools.reduce(jnp.maximum, parts, old)
        total = sout[at, :] * jnp.exp2(old - top)
        for part in parts:
            total += jnp.exp2(part - top)
        mout[at, :] = top
        sout[at, :] = total


def student_logits(where, scale, images, texts):
    rows = images[0].shape[0] // 2 * 8
    code = images[0].shape[1]
    width = 8 * texts[0].shape[0]
    return pl.pallas_call(
        student_kernel,
        grid=(width // COLS,),
        out_shape=(
            shape((rows, width), F32),
            shape((rows, LANES), F32),
            shape((rows, LANES), F32),
        ),
        in_specs=[SMEM, SMEM] + [ANY] * 24,
        out_specs=(
            pl.BlockSpec((rows, COLS), lambda i: (0, i)),
            pl.BlockSpec((rows, LANES), lambda i: (0, 0)),
            pl.BlockSpec((rows, LANES), lambda i: (0, 0)),
        ),
        scratch_shapes=[
            pltpu.VMEM((rows, code), BF16),
            pltpu.VMEM((width, code), BF16),
            pltpu.SemaphoreType.DMA((8,)),
            pltpu.SemaphoreType.DMA((16,)),
        ],
        compiler_params=params(),
        cost_estimate=pl.CostEstimate(
            flops=2 * rows * width * code, bytes_accessed=4 * rows * width, transcendentals=0
        ),
        name="student_logits",
    )(where, scale, *images, *texts)


def teacher_images_kernel(*refs):
    images, held, raw, sem = refs[:8], *refs[8:]
    rows = raw.shape[1]
    copies = [
        pltpu.make_async_copy(images[n].at[pl.ds(rows, rows), :], raw.at[n], sem.at[n])
        for n in range(8)
    ]
    for copy in copies:
        copy.start()
    for copy in copies:
        copy.wait()

    def block(l, carry):
        at = pl.ds(pl.multiple_of(l * LANES, LANES), LANES)
        values = [raw[n, :, at].astype(F32) for n in range(8)]
        square = sum(v * v for v in values)
        norm = jnp.sqrt(jnp.sum(square, axis=1, keepdims=True) + EPS)
        to = pl.ds(pl.multiple_of(l * rows, rows), rows)
        for n in range(8):
            held[to, n * LANES : (n + 1) * LANES] = (values[n] / norm).astype(BF16)
        return carry

    lax.fori_loop(0, 8, block, 0)


def teacher_images(images):
    rows, code = images[0].shape
    return pl.pallas_call(
        teacher_images_kernel,
        out_shape=shape((4 * rows, code), BF16),
        in_specs=[ANY] * 8,
        out_specs=VMEM,
        scratch_shapes=[pltpu.VMEM((8, rows // 2, code), BF16), pltpu.SemaphoreType.DMA((8,))],
        compiler_params=params(),
        name="teacher_images",
    )(*images)


def teacher_kernel(scale, *refs):
    held, texts = refs[0], refs[1:17]
    slog, ms, ss = refs[17:20]
    tlog, stats = refs[20:22]
    text, mt, st, ct, sem_text = refs[22:]
    step = pl.program_id(0)
    rows = held.shape[0] // 8
    text_copies = fetch_texts(texts, text, sem_text, rows, 1)

    @pl.when(step == 0)
    def _():
        for copy in text_copies:
            copy.start()
        mt[...] = jnp.full(mt.shape, -1e30, F32)
        st[...] = jnp.zeros(st.shape, F32)
        ct[...] = jnp.zeros(ct.shape, F32)

    wait_texts(text_copies, step, COLS, rows)
    factor = scale[0] * LOG2E
    cols = text[pl.ds(pl.multiple_of(step * COLS, COLS), COLS), :]

    for r in range(held.shape[0] // ROW_TILE):
        at = pl.ds(r * ROW_TILE, ROW_TILE)
        t = factor * lax.dot_general(
            held[at, :], cols, (((1,), (1,)), ((), ())), preferred_element_type=F32
        )
        tlog[at, :] = t
        s_parts = lanes_of(slog[at, :])
        t_parts = lanes_of(t)
        old = mt[at, :]
        top = functools.reduce(jnp.maximum, t_parts, old)
        shrink = jnp.exp2(old - top)
        total = st[at, :] * shrink
        cross = ct[at, :] * shrink
        for a, b in zip(t_parts, s_parts):
            e = jnp.exp2(a - top)
            total += e
            cross += e * (a - b)
        mt[at, :] = top
        st[at, :] = total
        ct[at, :] = cross

    @pl.when(step == pl.num_programs(0) - 1)
    def _():
        smax = jnp.max(ms[...], axis=1, keepdims=True)
        ssum = jnp.sum(ss[...] * jnp.exp2(ms[...] - smax), axis=1, keepdims=True)
        tmax = jnp.max(mt[...], axis=1, keepdims=True)
        shrink = jnp.exp2(mt[...] - tmax)
        tsum = jnp.sum(st[...] * shrink, axis=1, keepdims=True)
        cross = jnp.sum(ct[...] * shrink, axis=1, keepdims=True)
        lane = lax.broadcasted_iota(jnp.int32, ms.shape, 1)
        packed = jnp.zeros(ms.shape, F32)
        for n, value in enumerate((smax, ssum, tmax, tsum, cross)):
            packed = jnp.where(lane == n, value, packed)
        for n in range(8):
            stats[n] = packed.T[:8, :]


def teacher_logits(scale, image, texts, slog, ms, ss):
    rows, width = slog.shape
    code = image.shape[1]
    whole = pl.BlockSpec((rows, LANES), lambda i: (0, 0))
    return pl.pallas_call(
        teacher_kernel,
        grid=(width // COLS,),
        out_shape=(shape((rows, width), F32), shape((8, 8, rows), F32)),
        in_specs=[SMEM, pl.BlockSpec((rows, code), lambda i: (0, 0))]
        + [ANY] * 16
        + [pl.BlockSpec((rows, COLS), lambda i: (0, i)), whole, whole],
        out_specs=(
            pl.BlockSpec((rows, COLS), lambda i: (0, i)),
            pl.BlockSpec((8, 8, rows), lambda i: (0, 0, 0)),
        ),
        scratch_shapes=[
            pltpu.VMEM((width, code), BF16),
            pltpu.VMEM((rows, LANES), F32),
            pltpu.VMEM((rows, LANES), F32),
            pltpu.VMEM((rows, LANES), F32),
            pltpu.SemaphoreType.DMA((16,)),
        ],
        compiler_params=params(),
        cost_estimate=pl.CostEstimate(
            flops=2 * rows * width * code, bytes_accessed=8 * rows * width, transcendentals=0
        ),
        name="teacher_logits",
    )(scale, image, *texts, slog, ms, ss)


def merge_stats(stats, lses, lset, loss):
    smax = jnp.max(stats[:, 0, :], axis=0, keepdims=True)
    ssum = jnp.sum(stats[:, 1, :] * jnp.exp2(stats[:, 0, :] - smax), axis=0, keepdims=True)
    tmax = jnp.max(stats[:, 2, :], axis=0, keepdims=True)
    shrink = jnp.exp2(stats[:, 2, :] - tmax)
    tsum = jnp.sum(stats[:, 3, :] * shrink, axis=0, keepdims=True)
    cross = jnp.sum(stats[:, 4, :] * shrink, axis=0, keepdims=True)
    lse_s = smax + jnp.log2(ssum)
    lse_t = tmax + jnp.log2(tsum)
    diverge = LN2 * (cross / tsum - lse_t + lse_s)
    loss[...] = jnp.full(loss.shape, jnp.sum(diverge), F32)
    rows = stats.shape[2]
    lses[...] = jnp.broadcast_to(lse_s, (LANES, rows)).T
    lset[...] = jnp.broadcast_to(lse_t, (LANES, rows)).T


GCOLS = 256


def grads_kernel(where, scale, *refs):
    images, texts = refs[:8], refs[8:24]
    slog, tlog, stats = refs[24:27]
    keep, away, dimg, two, two_other, loss = refs[27:33]
    held, text, grad, acc, low, lses, lset, sem_image, sem_text, sem_out = refs[33:]
    step = pl.program_id(0)
    steps = pl.num_programs(0)
    rows = held.shape[0] // 8
    image_copies = fetch_images(where, images, held, sem_image, rows)
    text_copies = fetch_texts(texts, text, sem_text, rows, 0)

    @pl.when(step == 0)
    def _():
        for copy in text_copies[:2] + image_copies + text_copies[2:]:
            copy.start()
        acc[...] = jnp.zeros(acc.shape, F32)
        merge_stats(stats, lses, lset, loss)
        for copy in image_copies:
            copy.wait()

    wait_texts(text_copies, step, GCOLS, rows)
    cols = text[pl.ds(pl.multiple_of(step * GCOLS, GCOLS), GCOLS), :]

    for r in range(held.shape[0] // ROW_TILE):
        at = pl.ds(r * ROW_TILE, ROW_TILE)
        ls, lt = lses[at, :], lset[at, :]
        parts = []
        for a, b in zip(lanes_of(slog[at, :]), lanes_of(tlog[at, :])):
            parts.append((scale[0] * (jnp.exp2(a - ls) - jnp.exp2(b - lt))).astype(BF16))
        g = jnp.concatenate(parts, axis=1)
        grad[at, :] = g
        acc[at, :] += jnp.dot(g, cols, preferred_element_type=F32)

    term = lax.dot_general(
        grad[...], held[...], (((0,), (0,)), ((), ())), preferred_element_type=F32
    ).astype(BF16)

    @pl.when(step < steps // 2)
    def _():
        keep[...] = term

    @pl.when(step >= steps // 2)
    def _():
        away[...] = term

    @pl.when(step == steps - 1)
    def _():
        low[...] = acc[...].astype(BF16)
        copies = []
        for n, (k, j) in enumerate(PAIRS):
            start = pl.multiple_of(place(where, k, j) * rows, rows)
            target = (two, two_other)[j] if k == 2 else dimg.at[pl.ds(n * rows, rows), :]
            copies.append(
                pltpu.make_async_copy(low.at[pl.ds(start, rows), :], target, sem_out.at[n])
            )
        for copy in copies:
            copy.start()
        for copy in copies:
            copy.wait()


def grads(where, scale, images, texts, slog, tlog, stats):
    rows, width = slog.shape
    code = images[0].shape[1]
    own = rows // 8
    steps = width // GCOLS
    half = steps // 2
    column = pl.BlockSpec((rows, GCOLS), lambda i: (0, i))
    return pl.pallas_call(
        grads_kernel,
        grid=(steps,),
        out_shape=(
            shape((width // 2, code), BF16),
            shape((width // 2, code), BF16),
            shape((rows, code), BF16),
            shape((own, code), BF16),
            shape((own, code), BF16),
            shape((8, LANES), F32),
        ),
        in_specs=[SMEM, SMEM]
        + [ANY] * 24
        + [column, column, pl.BlockSpec(stats.shape, lambda i: (0, 0, 0))],
        out_specs=(
            pl.BlockSpec((GCOLS, code), lambda i: (jnp.minimum(i, half - 1), 0)),
            pl.BlockSpec((GCOLS, code), lambda i: (jnp.maximum(i - half, 0), 0)),
            ANY,
            ANY,
            ANY,
            pl.BlockSpec((8, LANES), lambda i: (0, 0)),
        ),
        scratch_shapes=[
            pltpu.VMEM((rows, code), BF16),
            pltpu.VMEM((width, code), BF16),
            pltpu.VMEM((rows, GCOLS), BF16),
            pltpu.VMEM((rows, code), F32),
            pltpu.VMEM((rows, code), BF16),
            pltpu.VMEM((rows, LANES), F32),
            pltpu.VMEM((rows, LANES), F32),
            pltpu.SemaphoreType.DMA((8,)),
            pltpu.SemaphoreType.DMA((16,)),
            pltpu.SemaphoreType.DMA((8,)),
        ],
        compiler_params=params(),
        cost_estimate=pl.CostEstimate(
            flops=4 * rows * width * code, bytes_accessed=8 * rows * width, transcendentals=0
        ),
        name="grads",
    )(where, scale, *images, *texts, slog, tlog, stats)


def on_device(
    student_image, student_text, teacher_image, teacher_text, student_scale, teacher_scale
):
    rows = student_image.shape[0]
    loop = lax.axis_index("loop")
    where = jnp.stack([loop // 2, loop % 2]).astype(jnp.int32)

    parts = lax.all_to_all(
        teacher_text.reshape(8, rows, -1), "loop", split_axis=0, concat_axis=0
    )
    image_own = own_image(student_image, teacher_image)
    x_first = ring_own(image_own, "x", "yl")
    text_own = own_text(where, student_text, parts)
    z_first = ring_own(text_own, "z", "yh")
    x_second = ring_other(x_first[2], "x")
    z_second = ring_other(tie(z_first[2], x_first), "z")
    x_third = ring_far(x_first[0], x_second[1], "x")
    z_third = ring_far(*tie((z_first[0], z_second[1]), x_second), "z")
    images = in_order(image_own, x_first, x_second, x_third)
    timg = teacher_images(images)
    mine = in_order(text_own, z_first, z_second, tie(z_third, timg))
    texts = mine + [send(v, core=1) for v in mine]

    slog, ms, ss = student_logits(where, student_scale, images, texts)
    tlog, stats = teacher_logits(teacher_scale, timg, texts, slog, ms, ss)
    stats = lax.all_to_all(stats, "loop", split_axis=0, concat_axis=0)
    keep, away, dimg, two, two_other, total = grads(
        where, student_scale, images, texts, slog, tlog, stats
    )
    got = send(away, core=1)
    totals = lax.all_to_all(
        jnp.broadcast_to(total[None], (16, *total.shape)), "row", split_axis=0, concat_axis=0
    )
    loss = (jnp.sum(totals[:, 0, 0]) / (rows * 128)).reshape(1)

    def scatter(terms, two, two_other, ring, pair, codes, after=()):
        ahead, behind = ring_add(
            terms, send(two, **{ring: 1}), send(two_other, **{ring: -1})
        )
        near = tie((send(ahead, **{ring: 1}), send(behind, **{ring: -1})), after)
        return finish(terms, near, send(pair_sum(terms, near), **{pair: 1}), codes)

    grad_image = scatter((dimg,), two, two_other, "x", "yl", student_image, totals)
    terms = (keep, got)
    grad_text = scatter(terms, *far_sum(terms), "z", "yh", student_text)
    return loss, grad_image, grad_text


def solution(mesh):
    return jax.shard_map(
        on_device,
        mesh=mesh,
        in_specs=(
            P(("row", "loop"), None),
            P(("row", "loop"), None),
            P("row", "loop"),
            P("row", "loop"),
            P(),
            P(),
        ),
        out_specs=(P(), P(("row", "loop"), None), P(("row", "loop"), None)),
        check_vma=False,
    )
```

```python
import functools
import math

import jax
import jax.numpy as jnp
from jax import lax
from jax.experimental import pallas as pl
from jax.experimental.pallas import tpu as pltpu
from jax.sharding import PartitionSpec as P

EPS = 1e-06
AXES = ("row", "loop")
SIZES = {"z": 4, "yh": 2, "core": 2, "x": 4, "yl": 2}
F32, BF16 = jnp.float32, jnp.bfloat16
LOG2E = math.log2(math.e)
LN2 = math.log(2.0)
LANES = 128
VMEM_LIMIT = 60 * 2**20
PAIRS = [(k, j) for k in range(4) for j in range(2)]
VMEM = pl.BlockSpec(memory_space=pltpu.VMEM)
SMEM = pl.BlockSpec(memory_space=pltpu.SMEM)
ANY = pl.BlockSpec(memory_space=pl.ANY)


def index_of(pos):
    index = 0
    for name, size in SIZES.items():
        index = index * size + pos[name] % size
    return index


def positions():
    found = [{}]
    for name, size in SIZES.items():
        found = [{**pos, name: i} for pos in found for i in range(size)]
    return found


def send(value, **step):
    perm = []
    for pos in positions():
        to = dict(pos)
        for name, by in step.items():
            to[name] = pos[name] + by
        perm.append((index_of(pos), index_of(to)))
    return lax.ppermute(value, AXES, perm=perm)


def swap_bit(value, axis, bit):
    perm = []
    for pos in positions():
        perm.append((index_of(pos), index_of({**pos, axis: pos[axis] ^ bit})))
    return lax.ppermute(value, AXES, perm=perm)


def params(**kw):
    return pltpu.CompilerParams(vmem_limit_bytes=VMEM_LIMIT, **kw)


def shape(dims, dtype):
    return jax.ShapeDtypeStruct(dims, dtype)


def norm_of(values):
    return jnp.sqrt(jnp.sum(values * values, axis=1, keepdims=True) + EPS)


def unit(codes):
    values = codes.astype(F32)
    return (values / norm_of(values)).astype(BF16)


def place(where_ref, k, j):
    return lax.rem(where_ref[0] + k, 4) * 2 + lax.rem(where_ref[1] + j, 2)


def own_kernel(si, ti, image):
    rows = si.shape[0]
    image[:rows, :] = unit(si[...])
    width = ti.shape[1]
    for l in range(8):
        image[rows:, l * width : (l + 1) * width] = ti[l * rows : (l + 1) * rows, :]


def own_image(si, ti):
    rows, code = si.shape
    return pl.pallas_call(
        own_kernel,
        out_shape=shape((2 * rows, code), BF16),
        in_specs=[VMEM] * 2,
        out_specs=VMEM,
        compiler_params=params(),
        name="own_image",
    )(si, ti)


def own_text_kernel(where, st, parts, text):
    rows = st.shape[0]
    text[:rows, :] = unit(st[...])
    values = jnp.concatenate([parts[place(where, k, j)] for k, j in PAIRS], axis=1)
    text[rows:, :] = unit(values)


def own_text(where, st, parts):
    rows, code = st.shape
    return pl.pallas_call(
        own_text_kernel,
        out_shape=shape((2 * rows, code), BF16),
        in_specs=[SMEM, VMEM, VMEM],
        out_specs=VMEM,
        compiler_params=params(),
        name="own_text",
    )(where, st, parts)


def tie(values, after):
    return lax.optimization_barrier((values, after))[0]


def ring_own(own, ring, pair):
    return send(own, **{ring: 1}), send(own, **{ring: -1}), send(own, **{pair: 1})


def ring_other(other, ring):
    return send(other, **{ring: 1}), send(other, **{ring: -1})


def ring_far(before, after_other, ring):
    return send(before, **{ring: 1}), send(after_other, **{ring: -1})


def in_order(own, first, second, third):
    before, after, other = first
    before_other, after_other = second
    far, far_other = third
    return [own, other, after, after_other, far, far_other, before, before_other]


def sum_of(refs):
    return sum(ref[...].astype(F32) for ref in refs)


def block_of(term, blocks, index):
    rows, code = term.shape
    return pl.BlockSpec((rows // blocks, code), lambda i: (index, 0))


def far_sum_kernel(n, *refs):
    two, two_other = refs[2 * n :]
    two[...] = sum_of(refs[:n]).astype(BF16)
    two_other[...] = sum_of(refs[n : 2 * n]).astype(BF16)


def far_sum(terms):
    n = len(terms)
    rows, code = terms[0].shape
    out = pl.BlockSpec((rows // 8, code), lambda i: (0, 0))
    return pl.pallas_call(
        functools.partial(far_sum_kernel, n),
        grid=(1,),
        out_shape=(shape((rows // 8, code), BF16),) * 2,
        in_specs=[block_of(t, 8, 4) for t in terms] + [block_of(t, 8, 5) for t in terms],
        out_specs=(out,) * 2,
        compiler_params=params(),
        name="far_sum",
    )(*terms, *terms)


def ring_add_kernel(n, *refs):
    to_next, to_prev, ahead, behind = refs[2 * n :]
    rows = to_next.shape[0]
    one = sum_of(refs[:n])
    three = sum_of(refs[n : 2 * n])
    ahead[:rows, :] = (one[:rows] + to_next[...].astype(F32)).astype(BF16)
    ahead[rows:, :] = one[rows:].astype(BF16)
    behind[:rows, :] = three[:rows].astype(BF16)
    behind[rows:, :] = (three[rows:] + to_prev[...].astype(F32)).astype(BF16)


def ring_add(terms, to_next, to_prev):
    n = len(terms)
    rows, code = to_next.shape
    half = pl.BlockSpec((rows, code), lambda i: (0, 0))
    out = pl.BlockSpec((2 * rows, code), lambda i: (0, 0))
    return pl.pallas_call(
        functools.partial(ring_add_kernel, n),
        grid=(1,),
        out_shape=(shape((2 * rows, code), BF16),) * 2,
        in_specs=[block_of(t, 4, 1) for t in terms]
        + [block_of(t, 4, 3) for t in terms]
        + [half, half],
        out_specs=(out,) * 2,
        compiler_params=params(),
        name="ring_add",
    )(*terms, *terms, to_next, to_prev)


def pair_sum_kernel(*refs):
    refs[-1][...] = sum_of(refs[:-1]).astype(BF16)


def pair_sum(terms, near):
    rows, code = near[0].shape
    return pl.pallas_call(
        pair_sum_kernel,
        grid=(1,),
        out_shape=shape((rows // 2, code), BF16),
        in_specs=[block_of(t, 8, 1) for t in terms] + [block_of(t, 2, 1) for t in near],
        out_specs=pl.BlockSpec((rows // 2, code), lambda i: (0, 0)),
        compiler_params=params(),
        name="pair_sum",
    )(*terms, *near)


def final_kernel(*refs):
    codes, out = refs[-2:]
    total = sum_of(refs[:-2])
    values = codes[...].astype(F32)
    norm = norm_of(values)
    units = values / norm
    inner = jnp.sum(total * units, axis=1, keepdims=True)
    out[...] = ((total - units * inner) / norm).astype(BF16)


def finish(terms, near, got, codes):
    own = pl.BlockSpec(codes.shape, lambda i: (0, 0))
    return pl.pallas_call(
        final_kernel,
        grid=(1,),
        out_shape=shape(codes.shape, BF16),
        in_specs=[own] * (len(terms) + len(near) + 2),
        out_specs=own,
        compiler_params=params(),
        name="finish",
    )(*terms, *near, got, codes)


def fetch_images(where, images, held, sem, rows):
    copies = []
    for n, (k, j) in enumerate(PAIRS):
        start = pl.multiple_of(place(where, k, j) * rows, rows)
        copies.append(
            pltpu.make_async_copy(
                images[n].at[pl.ds(0, rows), :], held.at[pl.ds(start, rows), :], sem.at[n]
            )
        )
    return copies


def fetch_texts(texts, held, sem, rows, part):
    return [
        pltpu.make_async_copy(
            texts[n].at[pl.ds(part * rows, rows), :], held.at[pl.ds(n * rows, rows), :], sem.at[n]
        )
        for n in range(16)
    ]


def wait_texts(copies, step, columns, rows):
    done = 0
    for at in range(16 * rows // columns):
        need = min(16, -(-(at + 1) * columns // rows))

        @pl.when(step == at)
        def _():
            for copy in copies[done:need]:
                copy.wait()

        done = need


ROW_TILE = 256
COLS = 512


def lanes_of(value):
    return [value[:, n * LANES : (n + 1) * LANES] for n in range(value.shape[1] // LANES)]


def student_kernel(where, scale, *refs):
    images, texts = refs[:8], refs[8:24]
    slog, mout, sout = refs[24:27]
    held, text, sem_image, sem_text = refs[27:]
    step = pl.program_id(0)
    rows = held.shape[0] // 8

    text_copies = fetch_texts(texts, text, sem_text, rows, 0)

    @pl.when(step == 0)
    def _():
        image_copies = fetch_images(where, images, held, sem_image, rows)
        for copy in image_copies + text_copies:
            copy.start()
        for copy in image_copies:
            copy.wait()
        mout[...] = jnp.full(mout.shape, -1e30, F32)
        sout[...] = jnp.zeros(sout.shape, F32)

    wait_texts(text_copies, step, COLS, rows)
    factor = scale[0] * LOG2E
    cols = text[pl.ds(pl.multiple_of(step * COLS, COLS), COLS), :]

    for r in range(held.shape[0] // ROW_TILE):
        at = pl.ds(r * ROW_TILE, ROW_TILE)
        s = factor * lax.dot_general(
            held[at, :], cols, (((1,), (1,)), ((), ())), preferred_element_type=F32
        )
        slog[at, :] = s
        old = mout[at, :]
        parts = lanes_of(s)
        top = functools.reduce(jnp.maximum, parts, old)
        total = sout[at, :] * jnp.exp2(old - top)
        for part in parts:
            total += jnp.exp2(part - top)
        mout[at, :] = top
        sout[at, :] = total


def student_logits(where, scale, images, texts):
    rows = images[0].shape[0] // 2 * 8
    code = images[0].shape[1]
    width = 8 * texts[0].shape[0]
    return pl.pallas_call(
        student_kernel,
        grid=(width // COLS,),
        out_shape=(
            shape((rows, width), F32),
            shape((rows, LANES), F32),
            shape((rows, LANES), F32),
        ),
        in_specs=[SMEM, SMEM] + [ANY] * 24,
        out_specs=(
            pl.BlockSpec((rows, COLS), lambda i: (0, i)),
            pl.BlockSpec((rows, LANES), lambda i: (0, 0)),
            pl.BlockSpec((rows, LANES), lambda i: (0, 0)),
        ),
        scratch_shapes=[
            pltpu.VMEM((rows, code), BF16),
            pltpu.VMEM((width, code), BF16),
            pltpu.SemaphoreType.DMA((8,)),
            pltpu.SemaphoreType.DMA((16,)),
        ],
        compiler_params=params(),
        cost_estimate=pl.CostEstimate(
            flops=2 * rows * width * code, bytes_accessed=4 * rows * width, transcendentals=0
        ),
        name="student_logits",
    )(where, scale, *images, *texts)


def teacher_images_kernel(*refs):
    images, held, raw, sem = refs[:8], *refs[8:]
    rows = raw.shape[1]
    copies = [
        pltpu.make_async_copy(images[n].at[pl.ds(rows, rows), :], raw.at[n], sem.at[n])
        for n in range(8)
    ]
    for copy in copies:
        copy.start()
    for copy in copies:
        copy.wait()

    def block(l, carry):
        at = pl.ds(pl.multiple_of(l * LANES, LANES), LANES)
        values = [raw[n, :, at].astype(F32) for n in range(8)]
        square = sum(v * v for v in values)
        norm = jnp.sqrt(jnp.sum(square, axis=1, keepdims=True) + EPS)
        to = pl.ds(pl.multiple_of(l * rows, rows), rows)
        for n in range(8):
            held[to, n * LANES : (n + 1) * LANES] = (values[n] / norm).astype(BF16)
        return carry

    lax.fori_loop(0, 8, block, 0)


def teacher_images(images):
    rows, code = images[0].shape
    return pl.pallas_call(
        teacher_images_kernel,
        out_shape=shape((4 * rows, code), BF16),
        in_specs=[ANY] * 8,
        out_specs=VMEM,
        scratch_shapes=[pltpu.VMEM((8, rows // 2, code), BF16), pltpu.SemaphoreType.DMA((8,))],
        compiler_params=params(),
        name="teacher_images",
    )(*images)


def teacher_kernel(scale, *refs):
    held, texts = refs[0], refs[1:17]
    slog, ms, ss = refs[17:20]
    tlog, stats = refs[20:22]
    text, mt, st, ct, sem_text = refs[22:]
    step = pl.program_id(0)
    rows = held.shape[0] // 8
    text_copies = fetch_texts(texts, text, sem_text, rows, 1)

    @pl.when(step == 0)
    def _():
        for copy in text_copies:
            copy.start()
        mt[...] = jnp.full(mt.shape, -1e30, F32)
        st[...] = jnp.zeros(st.shape, F32)
        ct[...] = jnp.zeros(ct.shape, F32)

    wait_texts(text_copies, step, COLS, rows)
    factor = scale[0] * LOG2E
    cols = text[pl.ds(pl.multiple_of(step * COLS, COLS), COLS), :]

    for r in range(held.shape[0] // ROW_TILE):
        at = pl.ds(r * ROW_TILE, ROW_TILE)
        t = factor * lax.dot_general(
            held[at, :], cols, (((1,), (1,)), ((), ())), preferred_element_type=F32
        )
        tlog[at, :] = t
        s_parts = lanes_of(slog[at, :])
        t_parts = lanes_of(t)
        old = mt[at, :]
        top = functools.reduce(jnp.maximum, t_parts, old)
        shrink = jnp.exp2(old - top)
        total = st[at, :] * shrink
        cross = ct[at, :] * shrink
        for a, b in zip(t_parts, s_parts):
            e = jnp.exp2(a - top)
            total += e
            cross += e * (a - b)
        mt[at, :] = top
        st[at, :] = total
        ct[at, :] = cross

    @pl.when(step == pl.num_programs(0) - 1)
    def _():
        smax = jnp.max(ms[...], axis=1, keepdims=True)
        ssum = jnp.sum(ss[...] * jnp.exp2(ms[...] - smax), axis=1, keepdims=True)
        tmax = jnp.max(mt[...], axis=1, keepdims=True)
        shrink = jnp.exp2(mt[...] - tmax)
        tsum = jnp.sum(st[...] * shrink, axis=1, keepdims=True)
        cross = jnp.sum(ct[...] * shrink, axis=1, keepdims=True)
        lane = lax.broadcasted_iota(jnp.int32, ms.shape, 1)
        packed = jnp.zeros(ms.shape, F32)
        for n, value in enumerate((smax, ssum, tmax, tsum, cross)):
            packed = jnp.where(lane == n, value, packed)
        for n in range(8):
            stats[n] = packed.T[:8, :]


def teacher_logits(scale, image, texts, slog, ms, ss):
    rows, width = slog.shape
    code = image.shape[1]
    whole = pl.BlockSpec((rows, LANES), lambda i: (0, 0))
    return pl.pallas_call(
        teacher_kernel,
        grid=(width // COLS,),
        out_shape=(shape((rows, width), F32), shape((8, 8, rows), F32)),
        in_specs=[SMEM, pl.BlockSpec((rows, code), lambda i: (0, 0))]
        + [ANY] * 16
        + [pl.BlockSpec((rows, COLS), lambda i: (0, i)), whole, whole],
        out_specs=(
            pl.BlockSpec((rows, COLS), lambda i: (0, i)),
            pl.BlockSpec((8, 8, rows), lambda i: (0, 0, 0)),
        ),
        scratch_shapes=[
            pltpu.VMEM((width, code), BF16),
            pltpu.VMEM((rows, LANES), F32),
            pltpu.VMEM((rows, LANES), F32),
            pltpu.VMEM((rows, LANES), F32),
            pltpu.SemaphoreType.DMA((16,)),
        ],
        compiler_params=params(),
        cost_estimate=pl.CostEstimate(
            flops=2 * rows * width * code, bytes_accessed=8 * rows * width, transcendentals=0
        ),
        name="teacher_logits",
    )(scale, image, *texts, slog, ms, ss)


def merge_stats(stats, lses, lset, loss):
    smax = jnp.max(stats[:, 0, :], axis=0, keepdims=True)
    ssum = jnp.sum(stats[:, 1, :] * jnp.exp2(stats[:, 0, :] - smax), axis=0, keepdims=True)
    tmax = jnp.max(stats[:, 2, :], axis=0, keepdims=True)
    shrink = jnp.exp2(stats[:, 2, :] - tmax)
    tsum = jnp.sum(stats[:, 3, :] * shrink, axis=0, keepdims=True)
    cross = jnp.sum(stats[:, 4, :] * shrink, axis=0, keepdims=True)
    lse_s = smax + jnp.log2(ssum)
    lse_t = tmax + jnp.log2(tsum)
    diverge = LN2 * (cross / tsum - lse_t + lse_s)
    loss[...] = jnp.full(loss.shape, jnp.sum(diverge), F32)
    rows = stats.shape[2]
    lses[...] = jnp.broadcast_to(lse_s, (LANES, rows)).T
    lset[...] = jnp.broadcast_to(lse_t, (LANES, rows)).T


GCOLS = 256


def grads_kernel(where, scale, *refs):
    images, texts = refs[:8], refs[8:24]
    slog, tlog, stats = refs[24:27]
    keep, away, dimg, two, two_other, loss = refs[27:33]
    held, text, grad, acc, low, lses, lset, sem_image, sem_text, sem_out = refs[33:]
    step = pl.program_id(0)
    steps = pl.num_programs(0)
    rows = held.shape[0] // 8
    image_copies = fetch_images(where, images, held, sem_image, rows)
    text_copies = fetch_texts(texts, text, sem_text, rows, 0)

    @pl.when(step == 0)
    def _():
        for copy in text_copies[:2] + image_copies + text_copies[2:]:
            copy.start()
        acc[...] = jnp.zeros(acc.shape, F32)
        merge_stats(stats, lses, lset, loss)
        for copy in image_copies:
            copy.wait()

    wait_texts(text_copies, step, GCOLS, rows)
    cols = text[pl.ds(pl.multiple_of(step * GCOLS, GCOLS), GCOLS), :]

    for r in range(held.shape[0] // ROW_TILE):
        at = pl.ds(r * ROW_TILE, ROW_TILE)
        ls, lt = lses[at, :], lset[at, :]
        parts = []
        for a, b in zip(lanes_of(slog[at, :]), lanes_of(tlog[at, :])):
            parts.append((scale[0] * (jnp.exp2(a - ls) - jnp.exp2(b - lt))).astype(BF16))
        g = jnp.concatenate(parts, axis=1)
        grad[at, :] = g
        acc[at, :] += jnp.dot(g, cols, preferred_element_type=F32)

    term = lax.dot_general(
        grad[...], held[...], (((0,), (0,)), ((), ())), preferred_element_type=F32
    ).astype(BF16)

    @pl.when(step < steps // 2)
    def _():
        keep[...] = term

    @pl.when(step >= steps // 2)
    def _():
        away[...] = term

    @pl.when(step == steps - 1)
    def _():
        low[...] = acc[...].astype(BF16)
        copies = []
        for n, (k, j) in enumerate(PAIRS):
            start = pl.multiple_of(place(where, k, j) * rows, rows)
            target = (two, two_other)[j] if k == 2 else dimg.at[pl.ds(n * rows, rows), :]
            copies.append(
                pltpu.make_async_copy(low.at[pl.ds(start, rows), :], target, sem_out.at[n])
            )
        for copy in copies:
            copy.start()
        for copy in copies:
            copy.wait()


def grads(where, scale, images, texts, slog, tlog, stats):
    rows, width = slog.shape
    code = images[0].shape[1]
    own = rows // 8
    steps = width // GCOLS
    half = steps // 2
    column = pl.BlockSpec((rows, GCOLS), lambda i: (0, i))
    return pl.pallas_call(
        grads_kernel,
        grid=(steps,),
        out_shape=(
            shape((width // 2, code), BF16),
            shape((width // 2, code), BF16),
            shape((rows, code), BF16),
            shape((own, code), BF16),
            shape((own, code), BF16),
            shape((8, LANES), F32),
        ),
        in_specs=[SMEM, SMEM]
        + [ANY] * 24
        + [column, column, pl.BlockSpec(stats.shape, lambda i: (0, 0, 0))],
        out_specs=(
            pl.BlockSpec((GCOLS, code), lambda i: (jnp.minimum(i, half - 1), 0)),
            pl.BlockSpec((GCOLS, code), lambda i: (jnp.maximum(i - half, 0), 0)),
            ANY,
            ANY,
            ANY,
            pl.BlockSpec((8, LANES), lambda i: (0, 0)),
        ),
        scratch_shapes=[
            pltpu.VMEM((rows, code), BF16),
            pltpu.VMEM((width, code), BF16),
            pltpu.VMEM((rows, GCOLS), BF16),
            pltpu.VMEM((rows, code), F32),
            pltpu.VMEM((rows, code), BF16),
            pltpu.VMEM((rows, LANES), F32),
            pltpu.VMEM((rows, LANES), F32),
            pltpu.SemaphoreType.DMA((8,)),
            pltpu.SemaphoreType.DMA((16,)),
            pltpu.SemaphoreType.DMA((8,)),
        ],
        compiler_params=params(),
        cost_estimate=pl.CostEstimate(
            flops=4 * rows * width * code, bytes_accessed=8 * rows * width, transcendentals=0
        ),
        name="grads",
    )(where, scale, *images, *texts, slog, tlog, stats)


def on_device(
    student_image, student_text, teacher_image, teacher_text, student_scale, teacher_scale
):
    rows = student_image.shape[0]
    loop = lax.axis_index("loop")
    where = jnp.stack([loop // 2, loop % 2]).astype(jnp.int32)

    parts = lax.all_to_all(
        teacher_text.reshape(8, rows, -1), "loop", split_axis=0, concat_axis=0
    )
    image_own = tie(own_image(student_image, teacher_image), parts)
    x_first = ring_own(image_own, "x", "yl")
    text_own = own_text(where, student_text, parts)
    z_first = ring_own(text_own, "z", "yh")
    x_second = ring_other(tie(x_first[2], x_first), "x")
    z_second = ring_other(tie(z_first[2], (x_first, z_first)), "z")
    x_third = ring_far(*tie((x_first[0], x_second[1]), (x_second, z_first)), "x")
    z_third = ring_far(*tie((z_first[0], z_second[1]), (x_second, z_second)), "z")
    images = in_order(image_own, x_first, x_second, x_third)
    timg = teacher_images(images)
    mine = in_order(text_own, z_first, z_second, tie(z_third, timg))
    texts = mine + [send(v, core=1) for v in mine]

    slog, ms, ss = student_logits(where, student_scale, images, texts)
    tlog, stats = teacher_logits(teacher_scale, timg, texts, slog, ms, ss)
    stats = lax.all_to_all(stats, "loop", split_axis=0, concat_axis=0)
    keep, away, dimg, two, two_other, total = grads(
        where, student_scale, images, texts, slog, tlog, stats
    )
    got = send(away, core=1)
    totals = []
    for axis, bit in (("core", 1), ("yh", 1), ("z", 1), ("z", 2)):
        total = total + swap_bit(total, axis, bit)
        totals.append(total)
    loss = (total[0, 0] / (rows * 128)).reshape(1)

    def scatter(terms, two, two_other, ring, pair, codes, after, last):
        ahead, behind = ring_add(
            terms, send(two, **{ring: 1}), send(two_other, **{ring: -1})
        )
        near = tie((send(ahead, **{ring: 1}), send(behind, **{ring: -1})), after)
        got = tie(send(pair_sum(terms, near), **{pair: 1}), last)
        return finish(terms, near, got, codes)

    grad_image = scatter((dimg,), two, two_other, "x", "yl", student_image, totals[1], totals[3])
    terms = (keep, got)
    grad_text = scatter(terms, *far_sum(terms), "z", "yh", student_text, totals[2], ())
    return loss, grad_image, grad_text


def solution(mesh):
    return jax.shard_map(
        on_device,
        mesh=mesh,
        in_specs=(
            P(("row", "loop"), None),
            P(("row", "loop"), None),
            P("row", "loop"),
            P("row", "loop"),
            P(),
            P(),
        ),
        out_specs=(P(), P(("row", "loop"), None), P(("row", "loop"), None)),
        check_vma=False,
    )
```

```python
import functools
import math

import jax
import jax.numpy as jnp
from jax import lax
from jax.experimental import pallas as pl
from jax.experimental.pallas import tpu as pltpu
from jax.sharding import PartitionSpec as P

EPS = 1e-06
AXES = ("row", "loop")
SIZES = {"z": 4, "yh": 2, "core": 2, "x": 4, "yl": 2}
F32, BF16 = jnp.float32, jnp.bfloat16
LOG2E = math.log2(math.e)
LN2 = math.log(2.0)
LANES = 128
VMEM_LIMIT = 60 * 2**20
PAIRS = [(k, j) for k in range(4) for j in range(2)]
VMEM = pl.BlockSpec(memory_space=pltpu.VMEM)
SMEM = pl.BlockSpec(memory_space=pltpu.SMEM)
ANY = pl.BlockSpec(memory_space=pl.ANY)


def index_of(pos):
    index = 0
    for name, size in SIZES.items():
        index = index * size + pos[name] % size
    return index


def positions():
    found = [{}]
    for name, size in SIZES.items():
        found = [{**pos, name: i} for pos in found for i in range(size)]
    return found


def send(value, **step):
    perm = []
    for pos in positions():
        to = dict(pos)
        for name, by in step.items():
            to[name] = pos[name] + by
        perm.append((index_of(pos), index_of(to)))
    return lax.ppermute(value, AXES, perm=perm)


def swap_bit(value, axis, bit):
    perm = []
    for pos in positions():
        perm.append((index_of(pos), index_of({**pos, axis: pos[axis] ^ bit})))
    return lax.ppermute(value, AXES, perm=perm)


def params(**kw):
    return pltpu.CompilerParams(vmem_limit_bytes=VMEM_LIMIT, **kw)


def shape(dims, dtype):
    return jax.ShapeDtypeStruct(dims, dtype)


def norm_of(values):
    return jnp.sqrt(jnp.sum(values * values, axis=1, keepdims=True) + EPS)


def unit(codes):
    values = codes.astype(F32)
    return (values / norm_of(values)).astype(BF16)


def place(where_ref, k, j):
    return lax.rem(where_ref[0] + k, 4) * 2 + lax.rem(where_ref[1] + j, 2)


def own_kernel(si, ti, image):
    rows = si.shape[0]
    image[:rows, :] = unit(si[...])
    width = ti.shape[1]
    for l in range(8):
        image[rows:, l * width : (l + 1) * width] = ti[l * rows : (l + 1) * rows, :]


def own_image(si, ti):
    rows, code = si.shape
    return pl.pallas_call(
        own_kernel,
        out_shape=shape((2 * rows, code), BF16),
        in_specs=[VMEM] * 2,
        out_specs=VMEM,
        compiler_params=params(),
        name="own_image",
    )(si, ti)


def own_text_kernel(where, st, parts, text):
    rows = st.shape[0]
    text[:rows, :] = unit(st[...])
    values = jnp.concatenate([parts[place(where, k, j)] for k, j in PAIRS], axis=1)
    text[rows:, :] = unit(values)


def own_text(where, st, parts):
    rows, code = st.shape
    return pl.pallas_call(
        own_text_kernel,
        out_shape=shape((2 * rows, code), BF16),
        in_specs=[SMEM, VMEM, VMEM],
        out_specs=VMEM,
        compiler_params=params(),
        name="own_text",
    )(where, st, parts)


def tie(values, after):
    return lax.optimization_barrier((values, after))[0]


def ring_own(own, ring, pair):
    return send(own, **{ring: 1}), send(own, **{ring: -1}), send(own, **{pair: 1})


def ring_other(other, ring):
    return send(other, **{ring: 1}), send(other, **{ring: -1})


def ring_far(before, after_other, ring):
    return send(before, **{ring: 1}), send(after_other, **{ring: -1})


def in_order(own, first, second, third):
    before, after, other = first
    before_other, after_other = second
    far, far_other = third
    return [own, other, after, after_other, far, far_other, before, before_other]


def sum_of(refs):
    return sum(ref[...].astype(F32) for ref in refs)


def block_of(term, blocks, index):
    rows, code = term.shape
    return pl.BlockSpec((rows // blocks, code), lambda i: (index, 0))


EARLY = (4, 5, 3, 6)
LATE = (2, 7)


def early_sum_kernel(n, *refs):
    for m in range(len(EARLY)):
        refs[n * len(EARLY) + m][...] = sum_of(refs[n * m : n * (m + 1)]).astype(BF16)


def early_sum(terms):
    n = len(terms)
    rows, code = terms[0].shape
    out = pl.BlockSpec((rows // 8, code), lambda i: (0, 0))
    return pl.pallas_call(
        functools.partial(early_sum_kernel, n),
        grid=(1,),
        out_shape=(shape((rows // 8, code), BF16),) * len(EARLY),
        in_specs=[block_of(t, 8, block) for block in EARLY for t in terms],
        out_specs=(out,) * len(EARLY),
        compiler_params=params(),
        name="early_sum",
    )(*(terms * len(EARLY)))


def ring_add_kernel(n, *refs):
    ahead, behind = refs[-2:]
    ahead[...] = sum_of(refs[: n + 1]).astype(BF16)
    behind[...] = sum_of(refs[n + 1 : 2 * n + 2]).astype(BF16)


def ring_add(terms, to_next, to_prev):
    n = len(terms)
    rows, code = to_next.shape
    own = pl.BlockSpec((rows, code), lambda i: (0, 0))
    return pl.pallas_call(
        functools.partial(ring_add_kernel, n),
        grid=(1,),
        out_shape=(shape((rows, code), BF16),) * 2,
        in_specs=[block_of(t, 8, LATE[0]) for t in terms]
        + [own]
        + [block_of(t, 8, LATE[1]) for t in terms]
        + [own],
        out_specs=(own,) * 2,
        compiler_params=params(),
        name="ring_add",
    )(*terms, to_next, *terms, to_prev)


def pair_sum_kernel(*refs):
    refs[-1][...] = sum_of(refs[:-1]).astype(BF16)


def pair_sum(terms, near):
    rows, code = near[0].shape
    own = pl.BlockSpec((rows, code), lambda i: (0, 0))
    return pl.pallas_call(
        pair_sum_kernel,
        grid=(1,),
        out_shape=shape((rows, code), BF16),
        in_specs=[block_of(t, 8, 1) for t in terms] + [own] * len(near),
        out_specs=own,
        compiler_params=params(),
        name="pair_sum",
    )(*terms, *near)


def final_kernel(*refs):
    codes, out = refs[-2:]
    total = sum_of(refs[:-2])
    values = codes[...].astype(F32)
    norm = norm_of(values)
    units = values / norm
    inner = jnp.sum(total * units, axis=1, keepdims=True)
    out[...] = ((total - units * inner) / norm).astype(BF16)


def finish(terms, near, got, codes):
    own = pl.BlockSpec(codes.shape, lambda i: (0, 0))
    return pl.pallas_call(
        final_kernel,
        grid=(1,),
        out_shape=shape(codes.shape, BF16),
        in_specs=[own] * (len(terms) + len(near) + 2),
        out_specs=own,
        compiler_params=params(),
        name="finish",
    )(*terms, *near, got, codes)


def fetch_images(where, images, held, sem, rows):
    copies = []
    for n, (k, j) in enumerate(PAIRS):
        start = pl.multiple_of(place(where, k, j) * rows, rows)
        copies.append(
            pltpu.make_async_copy(
                images[n].at[pl.ds(0, rows), :], held.at[pl.ds(start, rows), :], sem.at[n]
            )
        )
    return copies


def fetch_texts(texts, held, sem, rows, part):
    return [
        pltpu.make_async_copy(
            texts[n].at[pl.ds(part * rows, rows), :], held.at[pl.ds(n * rows, rows), :], sem.at[n]
        )
        for n in range(16)
    ]


def wait_texts(copies, step, columns, rows):
    done = 0
    for at in range(16 * rows // columns):
        need = min(16, -(-(at + 1) * columns // rows))

        @pl.when(step == at)
        def _():
            for copy in copies[done:need]:
                copy.wait()

        done = need


ROW_TILE = 256
COLS = 512


def lanes_of(value):
    return [value[:, n * LANES : (n + 1) * LANES] for n in range(value.shape[1] // LANES)]


def student_kernel(where, scale, *refs):
    images, texts = refs[:8], refs[8:24]
    slog, mout, sout = refs[24:27]
    held, text, sem_image, sem_text = refs[27:]
    step = pl.program_id(0)
    rows = held.shape[0] // 8

    text_copies = fetch_texts(texts, text, sem_text, rows, 0)

    @pl.when(step == 0)
    def _():
        image_copies = fetch_images(where, images, held, sem_image, rows)
        for copy in image_copies + text_copies:
            copy.start()
        for copy in image_copies:
            copy.wait()
        mout[...] = jnp.full(mout.shape, -1e30, F32)
        sout[...] = jnp.zeros(sout.shape, F32)

    wait_texts(text_copies, step, COLS, rows)
    factor = scale[0] * LOG2E
    cols = text[pl.ds(pl.multiple_of(step * COLS, COLS), COLS), :]

    for r in range(held.shape[0] // ROW_TILE):
        at = pl.ds(r * ROW_TILE, ROW_TILE)
        s = factor * lax.dot_general(
            held[at, :], cols, (((1,), (1,)), ((), ())), preferred_element_type=F32
        )
        slog[at, :] = s
        old = mout[at, :]
        parts = lanes_of(s)
        top = functools.reduce(jnp.maximum, parts, old)
        total = sout[at, :] * jnp.exp2(old - top)
        for part in parts:
            total += jnp.exp2(part - top)
        mout[at, :] = top
        sout[at, :] = total


def student_logits(where, scale, images, texts):
    rows = images[0].shape[0] // 2 * 8
    code = images[0].shape[1]
    width = 8 * texts[0].shape[0]
    return pl.pallas_call(
        student_kernel,
        grid=(width // COLS,),
        out_shape=(
            shape((rows, width), F32),
            shape((rows, LANES), F32),
            shape((rows, LANES), F32),
        ),
        in_specs=[SMEM, SMEM] + [ANY] * 24,
        out_specs=(
            pl.BlockSpec((rows, COLS), lambda i: (0, i)),
            pl.BlockSpec((rows, LANES), lambda i: (0, 0)),
            pl.BlockSpec((rows, LANES), lambda i: (0, 0)),
        ),
        scratch_shapes=[
            pltpu.VMEM((rows, code), BF16),
            pltpu.VMEM((width, code), BF16),
            pltpu.SemaphoreType.DMA((8,)),
            pltpu.SemaphoreType.DMA((16,)),
        ],
        compiler_params=params(),
        cost_estimate=pl.CostEstimate(
            flops=2 * rows * width * code, bytes_accessed=4 * rows * width, transcendentals=0
        ),
        name="student_logits",
    )(where, scale, *images, *texts)


def teacher_images_kernel(*refs):
    images, held, raw, sem = refs[:8], *refs[8:]
    rows = raw.shape[1]
    copies = [
        pltpu.make_async_copy(images[n].at[pl.ds(rows, rows), :], raw.at[n], sem.at[n])
        for n in range(8)
    ]
    for copy in copies:
        copy.start()
    for copy in copies:
        copy.wait()

    def block(l, carry):
        at = pl.ds(pl.multiple_of(l * LANES, LANES), LANES)
        values = [raw[n, :, at].astype(F32) for n in range(8)]
        square = sum(v * v for v in values)
        norm = jnp.sqrt(jnp.sum(square, axis=1, keepdims=True) + EPS)
        to = pl.ds(pl.multiple_of(l * rows, rows), rows)
        for n in range(8):
            held[to, n * LANES : (n + 1) * LANES] = (values[n] / norm).astype(BF16)
        return carry

    lax.fori_loop(0, 8, block, 0)


def teacher_images(images):
    rows, code = images[0].shape
    return pl.pallas_call(
        teacher_images_kernel,
        out_shape=shape((4 * rows, code), BF16),
        in_specs=[ANY] * 8,
        out_specs=VMEM,
        scratch_shapes=[pltpu.VMEM((8, rows // 2, code), BF16), pltpu.SemaphoreType.DMA((8,))],
        compiler_params=params(),
        name="teacher_images",
    )(*images)


def teacher_kernel(scale, *refs):
    held, texts = refs[0], refs[1:17]
    slog, ms, ss = refs[17:20]
    tlog, stats = refs[20:22]
    text, mt, st, ct, sem_text = refs[22:]
    step = pl.program_id(0)
    rows = held.shape[0] // 8
    text_copies = fetch_texts(texts, text, sem_text, rows, 1)

    @pl.when(step == 0)
    def _():
        for copy in text_copies:
            copy.start()
        mt[...] = jnp.full(mt.shape, -1e30, F32)
        st[...] = jnp.zeros(st.shape, F32)
        ct[...] = jnp.zeros(ct.shape, F32)

    wait_texts(text_copies, step, COLS, rows)
    factor = scale[0] * LOG2E
    cols = text[pl.ds(pl.multiple_of(step * COLS, COLS), COLS), :]

    for r in range(held.shape[0] // ROW_TILE):
        at = pl.ds(r * ROW_TILE, ROW_TILE)
        t = factor * lax.dot_general(
            held[at, :], cols, (((1,), (1,)), ((), ())), preferred_element_type=F32
        )
        tlog[at, :] = t
        s_parts = lanes_of(slog[at, :])
        t_parts = lanes_of(t)
        old = mt[at, :]
        top = functools.reduce(jnp.maximum, t_parts, old)
        shrink = jnp.exp2(old - top)
        total = st[at, :] * shrink
        cross = ct[at, :] * shrink
        for a, b in zip(t_parts, s_parts):
            e = jnp.exp2(a - top)
            total += e
            cross += e * (a - b)
        mt[at, :] = top
        st[at, :] = total
        ct[at, :] = cross

    @pl.when(step == pl.num_programs(0) - 1)
    def _():
        smax = jnp.max(ms[...], axis=1, keepdims=True)
        ssum = jnp.sum(ss[...] * jnp.exp2(ms[...] - smax), axis=1, keepdims=True)
        tmax = jnp.max(mt[...], axis=1, keepdims=True)
        shrink = jnp.exp2(mt[...] - tmax)
        tsum = jnp.sum(st[...] * shrink, axis=1, keepdims=True)
        cross = jnp.sum(ct[...] * shrink, axis=1, keepdims=True)
        lane = lax.broadcasted_iota(jnp.int32, ms.shape, 1)
        packed = jnp.zeros(ms.shape, F32)
        for n, value in enumerate((smax, ssum, tmax, tsum, cross)):
            packed = jnp.where(lane == n, value, packed)
        for n in range(8):
            stats[n] = packed.T[:8, :]


def teacher_logits(scale, image, texts, slog, ms, ss):
    rows, width = slog.shape
    code = image.shape[1]
    whole = pl.BlockSpec((rows, LANES), lambda i: (0, 0))
    return pl.pallas_call(
        teacher_kernel,
        grid=(width // COLS,),
        out_shape=(shape((rows, width), F32), shape((8, 8, rows), F32)),
        in_specs=[SMEM, pl.BlockSpec((rows, code), lambda i: (0, 0))]
        + [ANY] * 16
        + [pl.BlockSpec((rows, COLS), lambda i: (0, i)), whole, whole],
        out_specs=(
            pl.BlockSpec((rows, COLS), lambda i: (0, i)),
            pl.BlockSpec((8, 8, rows), lambda i: (0, 0, 0)),
        ),
        scratch_shapes=[
            pltpu.VMEM((width, code), BF16),
            pltpu.VMEM((rows, LANES), F32),
            pltpu.VMEM((rows, LANES), F32),
            pltpu.VMEM((rows, LANES), F32),
            pltpu.SemaphoreType.DMA((16,)),
        ],
        compiler_params=params(),
        cost_estimate=pl.CostEstimate(
            flops=2 * rows * width * code, bytes_accessed=8 * rows * width, transcendentals=0
        ),
        name="teacher_logits",
    )(scale, image, *texts, slog, ms, ss)


def merge_stats(stats, lses, lset, loss):
    smax = jnp.max(stats[:, 0, :], axis=0, keepdims=True)
    ssum = jnp.sum(stats[:, 1, :] * jnp.exp2(stats[:, 0, :] - smax), axis=0, keepdims=True)
    tmax = jnp.max(stats[:, 2, :], axis=0, keepdims=True)
    shrink = jnp.exp2(stats[:, 2, :] - tmax)
    tsum = jnp.sum(stats[:, 3, :] * shrink, axis=0, keepdims=True)
    cross = jnp.sum(stats[:, 4, :] * shrink, axis=0, keepdims=True)
    lse_s = smax + jnp.log2(ssum)
    lse_t = tmax + jnp.log2(tsum)
    diverge = LN2 * (cross / tsum - lse_t + lse_s)
    loss[...] = jnp.full(loss.shape, jnp.sum(diverge), F32)
    rows = stats.shape[2]
    lses[...] = jnp.broadcast_to(lse_s, (LANES, rows)).T
    lset[...] = jnp.broadcast_to(lse_t, (LANES, rows)).T


GCOLS = 256


def grads_kernel(where, scale, *refs):
    images, texts = refs[:8], refs[8:24]
    slog, tlog, stats = refs[24:27]
    keep, away, dimg, *early, loss = refs[27:35]
    held, text, grad, acc, low, lses, lset, sem_image, sem_text, sem_out = refs[35:]
    step = pl.program_id(0)
    steps = pl.num_programs(0)
    rows = held.shape[0] // 8
    image_copies = fetch_images(where, images, held, sem_image, rows)
    text_copies = fetch_texts(texts, text, sem_text, rows, 0)

    @pl.when(step == 0)
    def _():
        for copy in text_copies[:2] + image_copies + text_copies[2:]:
            copy.start()
        acc[...] = jnp.zeros(acc.shape, F32)
        merge_stats(stats, lses, lset, loss)
        for copy in image_copies:
            copy.wait()

    wait_texts(text_copies, step, GCOLS, rows)
    cols = text[pl.ds(pl.multiple_of(step * GCOLS, GCOLS), GCOLS), :]

    for r in range(held.shape[0] // ROW_TILE):
        at = pl.ds(r * ROW_TILE, ROW_TILE)
        ls, lt = lses[at, :], lset[at, :]
        parts = []
        for a, b in zip(lanes_of(slog[at, :]), lanes_of(tlog[at, :])):
            parts.append((scale[0] * (jnp.exp2(a - ls) - jnp.exp2(b - lt))).astype(BF16))
        g = jnp.concatenate(parts, axis=1)
        grad[at, :] = g
        acc[at, :] += jnp.dot(g, cols, preferred_element_type=F32)

    term = lax.dot_general(
        grad[...], held[...], (((0,), (0,)), ((), ())), preferred_element_type=F32
    ).astype(BF16)

    @pl.when(step < steps // 2)
    def _():
        keep[...] = term

    @pl.when(step >= steps // 2)
    def _():
        away[...] = term

    @pl.when(step == steps - 1)
    def _():
        low[...] = acc[...].astype(BF16)
        copies = []
        for n, (k, j) in enumerate(PAIRS):
            start = pl.multiple_of(place(where, k, j) * rows, rows)
            target = dimg.at[pl.ds(n * rows, rows), :]
            if n in EARLY:
                target = early[EARLY.index(n)]
            copies.append(
                pltpu.make_async_copy(low.at[pl.ds(start, rows), :], target, sem_out.at[n])
            )
        for copy in copies:
            copy.start()
        for copy in copies:
            copy.wait()


def grads(where, scale, images, texts, slog, tlog, stats):
    rows, width = slog.shape
    code = images[0].shape[1]
    own = rows // 8
    steps = width // GCOLS
    half = steps // 2
    column = pl.BlockSpec((rows, GCOLS), lambda i: (0, i))
    return pl.pallas_call(
        grads_kernel,
        grid=(steps,),
        out_shape=(
            shape((width // 2, code), BF16),
            shape((width // 2, code), BF16),
            shape((rows, code), BF16),
            *[shape((own, code), BF16)] * len(EARLY),
            shape((8, LANES), F32),
        ),
        in_specs=[SMEM, SMEM]
        + [ANY] * 24
        + [column, column, pl.BlockSpec(stats.shape, lambda i: (0, 0, 0))],
        out_specs=(
            pl.BlockSpec((GCOLS, code), lambda i: (jnp.minimum(i, half - 1), 0)),
            pl.BlockSpec((GCOLS, code), lambda i: (jnp.maximum(i - half, 0), 0)),
            *[ANY] * (1 + len(EARLY)),
            pl.BlockSpec((8, LANES), lambda i: (0, 0)),
        ),
        scratch_shapes=[
            pltpu.VMEM((rows, code), BF16),
            pltpu.VMEM((width, code), BF16),
            pltpu.VMEM((rows, GCOLS), BF16),
            pltpu.VMEM((rows, code), F32),
            pltpu.VMEM((rows, code), BF16),
            pltpu.VMEM((rows, LANES), F32),
            pltpu.VMEM((rows, LANES), F32),
            pltpu.SemaphoreType.DMA((8,)),
            pltpu.SemaphoreType.DMA((16,)),
            pltpu.SemaphoreType.DMA((8,)),
        ],
        compiler_params=params(),
        cost_estimate=pl.CostEstimate(
            flops=4 * rows * width * code, bytes_accessed=8 * rows * width, transcendentals=0
        ),
        name="grads",
    )(where, scale, *images, *texts, slog, tlog, stats)


def on_device(
    student_image, student_text, teacher_image, teacher_text, student_scale, teacher_scale
):
    rows = student_image.shape[0]
    loop = lax.axis_index("loop")
    where = jnp.stack([loop // 2, loop % 2]).astype(jnp.int32)

    parts = lax.all_to_all(
        teacher_text.reshape(8, rows, -1), "loop", split_axis=0, concat_axis=0
    )
    image_own = tie(own_image(student_image, teacher_image), parts)
    x_first = ring_own(image_own, "x", "yl")
    text_own = own_text(where, student_text, parts)
    z_first = ring_own(text_own, "z", "yh")
    x_second = ring_other(tie(x_first[2], x_first), "x")
    z_second = ring_other(tie(z_first[2], (x_first, z_first)), "z")
    x_third = ring_far(*tie((x_first[0], x_second[1]), (x_second, z_first)), "x")
    z_third = ring_far(*tie((z_first[0], z_second[1]), (x_second, z_second)), "z")
    images = in_order(image_own, x_first, x_second, x_third)
    timg = teacher_images(images)
    mine = in_order(text_own, z_first, z_second, tie(z_third, timg))
    texts = mine + [send(v, core=1) for v in mine]

    slog, ms, ss = student_logits(where, student_scale, images, texts)
    tlog, stats = teacher_logits(teacher_scale, timg, texts, slog, ms, ss)
    stats = lax.all_to_all(stats, "loop", split_axis=0, concat_axis=0)
    keep, away, dimg, *early, total = grads(
        where, student_scale, images, texts, slog, tlog, stats
    )
    got = send(away, core=1)

    def scatter(terms, early, ring):
        two, two_other, one_pair, three_own = early
        to_next = send(two, **{ring: 1})
        to_prev = send(two_other, **{ring: -1})
        pair_near = [send(one_pair, **{ring: 1})]
        own_near = [send(three_own, **{ring: -1})]
        ahead, behind = ring_add(terms, to_next, to_prev)
        own_near.append(send(ahead, **{ring: 1}))
        pair_near.append(send(behind, **{ring: -1}))
        return own_near, pair_near

    terms = (keep, got)
    x_own, x_pair = scatter((dimg,), early, "x")
    z_own, z_pair = scatter(terms, early_sum(terms), "z")
    for axis in ("core", "yh"):
        total = total + swap_bit(total, axis, 1)
    x_pair = tie(x_pair, total)
    x_got = send(pair_sum((dimg,), x_pair), yl=1)
    z_got = send(pair_sum(terms, z_pair), yh=1)
    total = tie(total, (z_own, z_pair))
    for bit in (1, 2):
        total = total + swap_bit(total, "z", bit)
    loss = (total[0, 0] / (rows * 128)).reshape(1)
    z_got = tie(z_got, total)
    return (
        loss,
        finish((dimg,), x_own, x_got, student_image),
        finish(terms, z_own, z_got, student_text),
    )


def solution(mesh):
    return jax.shard_map(
        on_device,
        mesh=mesh,
        in_specs=(
            P(("row", "loop"), None),
            P(("row", "loop"), None),
            P("row", "loop"),
            P("row", "loop"),
            P(),
            P(),
        ),
        out_specs=(P(), P(("row", "loop"), None), P(("row", "loop"), None)),
        check_vma=False,
    )
```

```python
import functools
import math

import jax
import jax.numpy as jnp
from jax import lax
from jax.experimental import pallas as pl
from jax.experimental.pallas import tpu as pltpu
from jax.sharding import PartitionSpec as P

EPS = 1e-06
AXES = ("row", "loop")
SIZES = {"z": 4, "yh": 2, "core": 2, "x": 4, "yl": 2}
F32, BF16 = jnp.float32, jnp.bfloat16
LOG2E = math.log2(math.e)
LN2 = math.log(2.0)
LANES = 128
VMEM_LIMIT = 64 * 2**20 - 2**18
PAIRS = [(k, j) for k in range(4) for j in range(2)]
VMEM = pl.BlockSpec(memory_space=pltpu.VMEM)
SMEM = pl.BlockSpec(memory_space=pltpu.SMEM)
ANY = pl.BlockSpec(memory_space=pl.ANY)


def index_of(pos):
    index = 0
    for name, size in SIZES.items():
        index = index * size + pos[name] % size
    return index


def positions():
    found = [{}]
    for name, size in SIZES.items():
        found = [{**pos, name: i} for pos in found for i in range(size)]
    return found


def send(value, **step):
    perm = []
    for pos in positions():
        to = dict(pos)
        for name, by in step.items():
            to[name] = pos[name] + by
        perm.append((index_of(pos), index_of(to)))
    return lax.ppermute(value, AXES, perm=perm)


def swap_bit(value, axis, bit):
    perm = []
    for pos in positions():
        perm.append((index_of(pos), index_of({**pos, axis: pos[axis] ^ bit})))
    return lax.ppermute(value, AXES, perm=perm)


def params(**kw):
    return pltpu.CompilerParams(vmem_limit_bytes=VMEM_LIMIT, **kw)


def shape(dims, dtype):
    return jax.ShapeDtypeStruct(dims, dtype)


def norm_of(values):
    return jnp.sqrt(jnp.sum(values * values, axis=1, keepdims=True) + EPS)


def unit(codes):
    values = codes.astype(F32)
    return (values / norm_of(values)).astype(BF16)


def place(where_ref, k, j):
    return lax.rem(where_ref[0] + k, 4) * 2 + lax.rem(where_ref[1] + j, 2)


def own_kernel(si, ti, image):
    rows = si.shape[0]
    image[:rows, :] = unit(si[...])
    width = ti.shape[1]
    for l in range(8):
        image[rows:, l * width : (l + 1) * width] = ti[l * rows : (l + 1) * rows, :]


def own_image(si, ti):
    rows, code = si.shape
    return pl.pallas_call(
        own_kernel,
        out_shape=shape((2 * rows, code), BF16),
        in_specs=[VMEM] * 2,
        out_specs=VMEM,
        compiler_params=params(),
        name="own_image",
    )(si, ti)


def own_text_kernel(where, st, parts, text):
    rows = st.shape[0]
    text[:rows, :] = unit(st[...])
    values = jnp.concatenate([parts[place(where, k, j)] for k, j in PAIRS], axis=1)
    text[rows:, :] = unit(values)


def own_text(where, st, parts):
    rows, code = st.shape
    return pl.pallas_call(
        own_text_kernel,
        out_shape=shape((2 * rows, code), BF16),
        in_specs=[SMEM, VMEM, VMEM],
        out_specs=VMEM,
        compiler_params=params(),
        name="own_text",
    )(where, st, parts)


def tie(values, after):
    return lax.optimization_barrier((values, after))[0]


def ring_own(own, ring, pair):
    return send(own, **{ring: 1}), send(own, **{ring: -1}), send(own, **{pair: 1})


def ring_other(other, ring):
    return send(other, **{ring: 1}), send(other, **{ring: -1})


def ring_far(before, after_other, ring):
    return send(before, **{ring: 1}), send(after_other, **{ring: -1})


def in_order(own, first, second, third):
    before, after, other = first
    before_other, after_other = second
    far, far_other = third
    return [own, other, after, after_other, far, far_other, before, before_other]


def sum_of(refs):
    return sum(ref[...].astype(F32) for ref in refs)


def block_of(term, blocks, index):
    rows, code = term.shape
    return pl.BlockSpec((rows // blocks, code), lambda i: (index, 0))


EARLY = (4, 5, 3, 6)
LATE = (2, 7)


def early_sum_kernel(n, *refs):
    for m in range(len(EARLY)):
        refs[n * len(EARLY) + m][...] = sum_of(refs[n * m : n * (m + 1)]).astype(BF16)


def early_sum(terms):
    n = len(terms)
    rows, code = terms[0].shape
    out = pl.BlockSpec((rows // 8, code), lambda i: (0, 0))
    return pl.pallas_call(
        functools.partial(early_sum_kernel, n),
        grid=(1,),
        out_shape=(shape((rows // 8, code), BF16),) * len(EARLY),
        in_specs=[block_of(t, 8, block) for block in EARLY for t in terms],
        out_specs=(out,) * len(EARLY),
        compiler_params=params(),
        name="early_sum",
    )(*(terms * len(EARLY)))


def ring_add_kernel(n, *refs):
    ahead, behind = refs[-2:]
    ahead[...] = sum_of(refs[: n + 1]).astype(BF16)
    behind[...] = sum_of(refs[n + 1 : 2 * n + 2]).astype(BF16)


def ring_add(terms, to_next, to_prev):
    n = len(terms)
    rows, code = to_next.shape
    own = pl.BlockSpec((rows, code), lambda i: (0, 0))
    return pl.pallas_call(
        functools.partial(ring_add_kernel, n),
        grid=(1,),
        out_shape=(shape((rows, code), BF16),) * 2,
        in_specs=[block_of(t, 8, LATE[0]) for t in terms]
        + [own]
        + [block_of(t, 8, LATE[1]) for t in terms]
        + [own],
        out_specs=(own,) * 2,
        compiler_params=params(),
        name="ring_add",
    )(*terms, to_next, *terms, to_prev)


def pair_sum_kernel(*refs):
    refs[-1][...] = sum_of(refs[:-1]).astype(BF16)


def pair_sum(terms, near):
    rows, code = near[0].shape
    own = pl.BlockSpec((rows, code), lambda i: (0, 0))
    return pl.pallas_call(
        pair_sum_kernel,
        grid=(1,),
        out_shape=shape((rows, code), BF16),
        in_specs=[block_of(t, 8, 1) for t in terms] + [own] * len(near),
        out_specs=own,
        compiler_params=params(),
        name="pair_sum",
    )(*terms, *near)


def final_kernel(*refs):
    codes, out = refs[-2:]
    total = sum_of(refs[:-2])
    values = codes[...].astype(F32)
    norm = norm_of(values)
    units = values / norm
    inner = jnp.sum(total * units, axis=1, keepdims=True)
    out[...] = ((total - units * inner) / norm).astype(BF16)


def finish(terms, near, got, codes):
    own = pl.BlockSpec(codes.shape, lambda i: (0, 0))
    return pl.pallas_call(
        final_kernel,
        grid=(1,),
        out_shape=shape(codes.shape, BF16),
        in_specs=[own] * (len(terms) + len(near) + 2),
        out_specs=own,
        compiler_params=params(),
        name="finish",
    )(*terms, *near, got, codes)


def fetch_images(where, images, held, sem, rows):
    copies = []
    for n, (k, j) in enumerate(PAIRS):
        start = pl.multiple_of(place(where, k, j) * rows, rows)
        copies.append(
            pltpu.make_async_copy(
                images[n].at[pl.ds(0, rows), :], held.at[pl.ds(start, rows), :], sem.at[n]
            )
        )
    return copies


def fetch_texts(texts, held, sem, rows, part):
    return [
        pltpu.make_async_copy(
            texts[n].at[pl.ds(part * rows, rows), :], held.at[pl.ds(n * rows, rows), :], sem.at[n]
        )
        for n in range(16)
    ]


def wait_texts(copies, step, columns, rows):
    done = 0
    for at in range(16 * rows // columns):
        need = min(16, -(-(at + 1) * columns // rows))

        @pl.when(step == at)
        def _():
            for copy in copies[done:need]:
                copy.wait()

        done = need


ROW_TILE = 256
COLS = 512


def lanes_of(value):
    return [value[:, n * LANES : (n + 1) * LANES] for n in range(value.shape[1] // LANES)]


def student_kernel(where, scale, *refs):
    images, texts = refs[:8], refs[8:24]
    slog, mout, sout = refs[24:27]
    held, text, sem_image, sem_text = refs[27:]
    step = pl.program_id(0)
    rows = held.shape[0] // 8

    text_copies = fetch_texts(texts, text, sem_text, rows, 0)

    @pl.when(step == 0)
    def _():
        image_copies = fetch_images(where, images, held, sem_image, rows)
        for copy in image_copies + text_copies:
            copy.start()
        for copy in image_copies:
            copy.wait()
        mout[...] = jnp.full(mout.shape, -1e30, F32)
        sout[...] = jnp.zeros(sout.shape, F32)

    wait_texts(text_copies, step, COLS, rows)
    factor = scale[0] * LOG2E
    cols = text[pl.ds(pl.multiple_of(step * COLS, COLS), COLS), :]

    for r in range(held.shape[0] // ROW_TILE):
        at = pl.ds(r * ROW_TILE, ROW_TILE)
        s = factor * lax.dot_general(
            held[at, :], cols, (((1,), (1,)), ((), ())), preferred_element_type=F32
        )
        slog[at, :] = s
        old = mout[at, :]
        parts = lanes_of(s)
        top = functools.reduce(jnp.maximum, parts, old)
        total = sout[at, :] * jnp.exp2(old - top)
        for part in parts:
            total += jnp.exp2(part - top)
        mout[at, :] = top
        sout[at, :] = total


def student_logits(where, scale, images, texts):
    rows = images[0].shape[0] // 2 * 8
    code = images[0].shape[1]
    width = 8 * texts[0].shape[0]
    return pl.pallas_call(
        student_kernel,
        grid=(width // COLS,),
        out_shape=(
            shape((rows, width), F32),
            shape((rows, LANES), F32),
            shape((rows, LANES), F32),
        ),
        in_specs=[SMEM, SMEM] + [ANY] * 24,
        out_specs=(
            pl.BlockSpec((rows, COLS), lambda i: (0, i)),
            pl.BlockSpec((rows, LANES), lambda i: (0, 0)),
            pl.BlockSpec((rows, LANES), lambda i: (0, 0)),
        ),
        scratch_shapes=[
            pltpu.VMEM((rows, code), BF16),
            pltpu.VMEM((width, code), BF16),
            pltpu.SemaphoreType.DMA((8,)),
            pltpu.SemaphoreType.DMA((16,)),
        ],
        compiler_params=params(),
        cost_estimate=pl.CostEstimate(
            flops=2 * rows * width * code, bytes_accessed=4 * rows * width, transcendentals=0
        ),
        name="student_logits",
    )(where, scale, *images, *texts)


def teacher_images_kernel(*refs):
    images, held, raw, sem = refs[:8], *refs[8:]
    rows = raw.shape[1]
    copies = [
        pltpu.make_async_copy(images[n].at[pl.ds(rows, rows), :], raw.at[n], sem.at[n])
        for n in range(8)
    ]
    for copy in copies:
        copy.start()
    for copy in copies:
        copy.wait()

    def block(l, carry):
        at = pl.ds(pl.multiple_of(l * LANES, LANES), LANES)
        values = [raw[n, :, at].astype(F32) for n in range(8)]
        square = sum(v * v for v in values)
        norm = jnp.sqrt(jnp.sum(square, axis=1, keepdims=True) + EPS)
        to = pl.ds(pl.multiple_of(l * rows, rows), rows)
        for n in range(8):
            held[to, n * LANES : (n + 1) * LANES] = (values[n] / norm).astype(BF16)
        return carry

    lax.fori_loop(0, 8, block, 0)


def teacher_images(images):
    rows, code = images[0].shape
    return pl.pallas_call(
        teacher_images_kernel,
        out_shape=shape((4 * rows, code), BF16),
        in_specs=[ANY] * 8,
        out_specs=VMEM,
        scratch_shapes=[pltpu.VMEM((8, rows // 2, code), BF16), pltpu.SemaphoreType.DMA((8,))],
        compiler_params=params(),
        name="teacher_images",
    )(*images)


def teacher_kernel(scale, *refs):
    held, texts = refs[0], refs[1:17]
    slog, ms, ss = refs[17:20]
    tlog, stats = refs[20:22]
    text, mt, st, ct, sem_text = refs[22:]
    step = pl.program_id(0)
    rows = held.shape[0] // 8
    text_copies = fetch_texts(texts, text, sem_text, rows, 1)

    @pl.when(step == 0)
    def _():
        for copy in text_copies:
            copy.start()
        mt[...] = jnp.full(mt.shape, -1e30, F32)
        st[...] = jnp.zeros(st.shape, F32)
        ct[...] = jnp.zeros(ct.shape, F32)

    wait_texts(text_copies, step, COLS, rows)
    factor = scale[0] * LOG2E
    cols = text[pl.ds(pl.multiple_of(step * COLS, COLS), COLS), :]

    for r in range(held.shape[0] // ROW_TILE):
        at = pl.ds(r * ROW_TILE, ROW_TILE)
        t = factor * lax.dot_general(
            held[at, :], cols, (((1,), (1,)), ((), ())), preferred_element_type=F32
        )
        tlog[at, :] = t
        s_parts = lanes_of(slog[at, :])
        t_parts = lanes_of(t)
        old = mt[at, :]
        top = functools.reduce(jnp.maximum, t_parts, old)
        shrink = jnp.exp2(old - top)
        total = st[at, :] * shrink
        cross = ct[at, :] * shrink
        for a, b in zip(t_parts, s_parts):
            e = jnp.exp2(a - top)
            total += e
            cross += e * (a - b)
        mt[at, :] = top
        st[at, :] = total
        ct[at, :] = cross

    @pl.when(step == pl.num_programs(0) - 1)
    def _():
        smax = jnp.max(ms[...], axis=1, keepdims=True)
        ssum = jnp.sum(ss[...] * jnp.exp2(ms[...] - smax), axis=1, keepdims=True)
        tmax = jnp.max(mt[...], axis=1, keepdims=True)
        shrink = jnp.exp2(mt[...] - tmax)
        tsum = jnp.sum(st[...] * shrink, axis=1, keepdims=True)
        cross = jnp.sum(ct[...] * shrink, axis=1, keepdims=True)
        lane = lax.broadcasted_iota(jnp.int32, ms.shape, 1)
        packed = jnp.zeros(ms.shape, F32)
        for n, value in enumerate((smax, ssum, tmax, tsum, cross)):
            packed = jnp.where(lane == n, value, packed)
        for n in range(8):
            stats[n] = packed.T[:8, :]


def teacher_logits(scale, image, texts, slog, ms, ss):
    rows, width = slog.shape
    code = image.shape[1]
    whole = pl.BlockSpec((rows, LANES), lambda i: (0, 0))
    return pl.pallas_call(
        teacher_kernel,
        grid=(width // COLS,),
        out_shape=(shape((rows, width), F32), shape((8, 8, rows), F32)),
        in_specs=[SMEM, pl.BlockSpec((rows, code), lambda i: (0, 0))]
        + [ANY] * 16
        + [pl.BlockSpec((rows, COLS), lambda i: (0, i)), whole, whole],
        out_specs=(
            pl.BlockSpec((rows, COLS), lambda i: (0, i)),
            pl.BlockSpec((8, 8, rows), lambda i: (0, 0, 0)),
        ),
        scratch_shapes=[
            pltpu.VMEM((width, code), BF16),
            pltpu.VMEM((rows, LANES), F32),
            pltpu.VMEM((rows, LANES), F32),
            pltpu.VMEM((rows, LANES), F32),
            pltpu.SemaphoreType.DMA((16,)),
        ],
        compiler_params=params(),
        cost_estimate=pl.CostEstimate(
            flops=2 * rows * width * code, bytes_accessed=8 * rows * width, transcendentals=0
        ),
        name="teacher_logits",
    )(scale, image, *texts, slog, ms, ss)


def merge_stats(stats, lses, lset, loss):
    smax = jnp.max(stats[:, 0, :], axis=0, keepdims=True)
    ssum = jnp.sum(stats[:, 1, :] * jnp.exp2(stats[:, 0, :] - smax), axis=0, keepdims=True)
    tmax = jnp.max(stats[:, 2, :], axis=0, keepdims=True)
    shrink = jnp.exp2(stats[:, 2, :] - tmax)
    tsum = jnp.sum(stats[:, 3, :] * shrink, axis=0, keepdims=True)
    cross = jnp.sum(stats[:, 4, :] * shrink, axis=0, keepdims=True)
    lse_s = smax + jnp.log2(ssum)
    lse_t = tmax + jnp.log2(tsum)
    diverge = LN2 * (cross / tsum - lse_t + lse_s)
    loss[...] = jnp.full(loss.shape, jnp.sum(diverge), F32)
    rows = stats.shape[2]
    lses[...] = jnp.broadcast_to(lse_s, (LANES, rows)).T
    lset[...] = jnp.broadcast_to(lse_t, (LANES, rows)).T


GCOLS = 256


def grads_kernel(where, scale, *refs):
    images, texts = refs[:8], refs[8:24]
    slog, tlog, stats = refs[24:27]
    keep, away, dimg, *early, loss = refs[27:35]
    held, text, grad, acc, low, lses, lset, sem_image, sem_text, sem_out = refs[35:]
    step = pl.program_id(0)
    steps = pl.num_programs(0)
    rows = held.shape[0] // 8
    image_copies = fetch_images(where, images, held, sem_image, rows)
    text_copies = fetch_texts(texts, text, sem_text, rows, 0)

    @pl.when(step == 0)
    def _():
        for copy in text_copies[:2] + image_copies + text_copies[2:]:
            copy.start()
        acc[...] = jnp.zeros(acc.shape, F32)
        merge_stats(stats, lses, lset, loss)
        for copy in image_copies:
            copy.wait()

    wait_texts(text_copies, step, GCOLS, rows)
    cols = text[pl.ds(pl.multiple_of(step * GCOLS, GCOLS), GCOLS), :]

    for r in range(held.shape[0] // ROW_TILE):
        at = pl.ds(r * ROW_TILE, ROW_TILE)
        ls, lt = lses[at, :], lset[at, :]
        parts = []
        for a, b in zip(lanes_of(slog[at, :]), lanes_of(tlog[at, :])):
            parts.append((scale[0] * (jnp.exp2(a - ls) - jnp.exp2(b - lt))).astype(BF16))
        g = jnp.concatenate(parts, axis=1)
        grad[at, :] = g
        acc[at, :] += jnp.dot(g, cols, preferred_element_type=F32)

    term = lax.dot_general(
        grad[...], held[...], (((0,), (0,)), ((), ())), preferred_element_type=F32
    ).astype(BF16)

    @pl.when(step < steps // 2)
    def _():
        keep[...] = term

    @pl.when(step >= steps // 2)
    def _():
        away[...] = term

    @pl.when(step == steps - 1)
    def _():
        low[...] = acc[...].astype(BF16)
        copies = []
        for n, (k, j) in enumerate(PAIRS):
            start = pl.multiple_of(place(where, k, j) * rows, rows)
            target = dimg.at[pl.ds(n * rows, rows), :]
            if n in EARLY:
                target = early[EARLY.index(n)]
            copies.append(
                pltpu.make_async_copy(low.at[pl.ds(start, rows), :], target, sem_out.at[n])
            )
        for copy in copies:
            copy.start()
        for copy in copies:
            copy.wait()


def grads(where, scale, images, texts, slog, tlog, stats):
    rows, width = slog.shape
    code = images[0].shape[1]
    own = rows // 8
    steps = width // GCOLS
    half = steps // 2
    column = pl.BlockSpec((rows, GCOLS), lambda i: (0, i))
    return pl.pallas_call(
        grads_kernel,
        grid=(steps,),
        out_shape=(
            shape((width // 2, code), BF16),
            shape((width // 2, code), BF16),
            shape((rows, code), BF16),
            *[shape((own, code), BF16)] * len(EARLY),
            shape((8, LANES), F32),
        ),
        in_specs=[SMEM, SMEM]
        + [ANY] * 24
        + [column, column, pl.BlockSpec(stats.shape, lambda i: (0, 0, 0))],
        out_specs=(
            pl.BlockSpec((GCOLS, code), lambda i: (jnp.minimum(i, half - 1), 0)),
            pl.BlockSpec((GCOLS, code), lambda i: (jnp.maximum(i - half, 0), 0)),
            *[ANY] * (1 + len(EARLY)),
            pl.BlockSpec((8, LANES), lambda i: (0, 0)),
        ),
        scratch_shapes=[
            pltpu.VMEM((rows, code), BF16),
            pltpu.VMEM((width, code), BF16),
            pltpu.VMEM((rows, GCOLS), BF16),
            pltpu.VMEM((rows, code), F32),
            pltpu.VMEM((rows, code), BF16),
            pltpu.VMEM((rows, LANES), F32),
            pltpu.VMEM((rows, LANES), F32),
            pltpu.SemaphoreType.DMA((8,)),
            pltpu.SemaphoreType.DMA((16,)),
            pltpu.SemaphoreType.DMA((8,)),
        ],
        compiler_params=params(),
        cost_estimate=pl.CostEstimate(
            flops=4 * rows * width * code, bytes_accessed=8 * rows * width, transcendentals=0
        ),
        name="grads",
    )(where, scale, *images, *texts, slog, tlog, stats)


def on_device(
    student_image, student_text, teacher_image, teacher_text, student_scale, teacher_scale
):
    rows = student_image.shape[0]
    loop = lax.axis_index("loop")
    where = jnp.stack([loop // 2, loop % 2]).astype(jnp.int32)

    parts = lax.all_to_all(
        teacher_text.reshape(8, rows, -1), "loop", split_axis=0, concat_axis=0
    )
    image_own = tie(own_image(student_image, teacher_image), parts)
    x_first = ring_own(image_own, "x", "yl")
    text_own = own_text(where, student_text, parts)
    z_first = ring_own(text_own, "z", "yh")
    x_second = ring_other(tie(x_first[2], x_first), "x")
    z_second = ring_other(tie(z_first[2], (x_first, z_first)), "z")
    x_third = ring_far(*tie((x_first[0], x_second[1]), (x_second, z_first)), "x")
    z_third = ring_far(*tie((z_first[0], z_second[1]), (x_second, z_second)), "z")
    images = in_order(image_own, x_first, x_second, x_third)
    timg = teacher_images(images)
    mine = in_order(text_own, z_first, z_second, tie(z_third, timg))
    texts = mine + [send(v, core=1) for v in mine]

    slog, ms, ss = student_logits(where, student_scale, images, texts)
    tlog, stats = teacher_logits(teacher_scale, timg, texts, slog, ms, ss)
    stats = lax.all_to_all(stats, "loop", split_axis=0, concat_axis=0)
    keep, away, dimg, *early, total = grads(
        where, student_scale, images, texts, slog, tlog, stats
    )
    got = send(away, core=1)

    def scatter(terms, early, ring):
        two, two_other, one_pair, three_own = early
        to_next = send(two, **{ring: 1})
        to_prev = send(two_other, **{ring: -1})
        pair_near = [send(one_pair, **{ring: 1})]
        own_near = [send(three_own, **{ring: -1})]
        ahead, behind = ring_add(terms, to_next, to_prev)
        own_near.append(send(ahead, **{ring: 1}))
        pair_near.append(send(behind, **{ring: -1}))
        return own_near, pair_near

    terms = (keep, got)
    x_own, x_pair = scatter((dimg,), early, "x")
    z_own, z_pair = scatter(terms, early_sum(terms), "z")
    for axis in ("core", "yh"):
        total = total + swap_bit(total, axis, 1)
    x_pair = tie(x_pair, total)
    x_got = send(pair_sum((dimg,), x_pair), yl=1)
    z_got = send(pair_sum(terms, z_pair), yh=1)
    total = tie(total, (z_own, z_pair))
    for bit in (1, 2):
        total = total + swap_bit(total, "z", bit)
    loss = (total[0, 0] / (rows * 128)).reshape(1)
    z_got = tie(z_got, total)
    return (
        loss,
        finish((dimg,), x_own, x_got, student_image),
        finish(terms, z_own, z_got, student_text),
    )


def solution(mesh):
    return jax.shard_map(
        on_device,
        mesh=mesh,
        in_specs=(
            P(("row", "loop"), None),
            P(("row", "loop"), None),
            P("row", "loop"),
            P("row", "loop"),
            P(),
            P(),
        ),
        out_specs=(P(), P(("row", "loop"), None), P(("row", "loop"), None)),
        check_vma=False,
    )
```

```python
import functools
import math

import jax
import jax.numpy as jnp
from jax import lax
from jax.experimental import pallas as pl
from jax.experimental.pallas import tpu as pltpu
from jax.sharding import PartitionSpec as P

EPS = 1e-06
AXES = ("row", "loop")
SIZES = {"z": 4, "yh": 2, "core": 2, "x": 4, "yl": 2}
F32, BF16 = jnp.float32, jnp.bfloat16
LOG2E = math.log2(math.e)
LN2 = math.log(2.0)
LANES = 128
VMEM_LIMIT = 64 * 2**20 - 2**18
PAIRS = [(k, j) for k in range(4) for j in range(2)]
VMEM = pl.BlockSpec(memory_space=pltpu.VMEM)
SMEM = pl.BlockSpec(memory_space=pltpu.SMEM)
ANY = pl.BlockSpec(memory_space=pl.ANY)


def index_of(pos):
    index = 0
    for name, size in SIZES.items():
        index = index * size + pos[name] % size
    return index


def positions():
    found = [{}]
    for name, size in SIZES.items():
        found = [{**pos, name: i} for pos in found for i in range(size)]
    return found


def send(value, **step):
    perm = []
    for pos in positions():
        to = dict(pos)
        for name, by in step.items():
            to[name] = pos[name] + by
        perm.append((index_of(pos), index_of(to)))
    return lax.ppermute(value, AXES, perm=perm)


def swap_bit(value, axis, bit):
    perm = []
    for pos in positions():
        perm.append((index_of(pos), index_of({**pos, axis: pos[axis] ^ bit})))
    return lax.ppermute(value, AXES, perm=perm)


def params(**kw):
    return pltpu.CompilerParams(vmem_limit_bytes=VMEM_LIMIT, **kw)


def shape(dims, dtype):
    return jax.ShapeDtypeStruct(dims, dtype)


def norm_of(values):
    return jnp.sqrt(jnp.sum(values * values, axis=1, keepdims=True) + EPS)


def unit(codes):
    values = codes.astype(F32)
    return (values / norm_of(values)).astype(BF16)


def place(where_ref, k, j):
    return lax.rem(where_ref[0] + k, 4) * 2 + lax.rem(where_ref[1] + j, 2)


def own_kernel(si, ti, image):
    rows = si.shape[0]
    image[:rows, :] = unit(si[...])
    width = ti.shape[1]
    for l in range(8):
        image[rows:, l * width : (l + 1) * width] = ti[l * rows : (l + 1) * rows, :]


def own_image(si, ti):
    rows, code = si.shape
    return pl.pallas_call(
        own_kernel,
        out_shape=shape((2 * rows, code), BF16),
        in_specs=[VMEM] * 2,
        out_specs=VMEM,
        compiler_params=params(),
        name="own_image",
    )(si, ti)


def own_text_kernel(where, st, parts, text):
    rows = st.shape[0]
    text[:rows, :] = unit(st[...])
    values = jnp.concatenate([parts[place(where, k, j)] for k, j in PAIRS], axis=1)
    text[rows:, :] = unit(values)


def own_text(where, st, parts):
    rows, code = st.shape
    return pl.pallas_call(
        own_text_kernel,
        out_shape=shape((2 * rows, code), BF16),
        in_specs=[SMEM, VMEM, VMEM],
        out_specs=VMEM,
        compiler_params=params(),
        name="own_text",
    )(where, st, parts)


def tie(values, after):
    return lax.optimization_barrier((values, after))[0]


def ring_own(own, ring, pair):
    return send(own, **{ring: 1}), send(own, **{ring: -1}), send(own, **{pair: 1})


def ring_other(other, ring):
    return send(other, **{ring: 1}), send(other, **{ring: -1})


def ring_far(before, after_other, ring):
    return send(before, **{ring: 1}), send(after_other, **{ring: -1})


def in_order(own, first, second, third):
    before, after, other = first
    before_other, after_other = second
    far, far_other = third
    return [own, other, after, after_other, far, far_other, before, before_other]


def sum_of(refs):
    return sum(ref[...].astype(F32) for ref in refs)


def block_of(term, blocks, index):
    rows, code = term.shape
    return pl.BlockSpec((rows // blocks, code), lambda i: (index, 0))


EARLY = (4, 5, 3, 6)
LATE = (2, 7)


def early_sum_kernel(n, *refs):
    for m in range(len(EARLY)):
        refs[n * len(EARLY) + m][...] = sum_of(refs[n * m : n * (m + 1)]).astype(BF16)


def early_sum(terms):
    n = len(terms)
    rows, code = terms[0].shape
    out = pl.BlockSpec((rows // 8, code), lambda i: (0, 0))
    return pl.pallas_call(
        functools.partial(early_sum_kernel, n),
        grid=(1,),
        out_shape=(shape((rows // 8, code), BF16),) * len(EARLY),
        in_specs=[block_of(t, 8, block) for block in EARLY for t in terms],
        out_specs=(out,) * len(EARLY),
        compiler_params=params(),
        name="early_sum",
    )(*(terms * len(EARLY)))


def ring_add_kernel(n, *refs):
    ahead, behind = refs[-2:]
    ahead[...] = sum_of(refs[: n + 1]).astype(BF16)
    behind[...] = sum_of(refs[n + 1 : 2 * n + 2]).astype(BF16)


def ring_add(terms, to_next, to_prev):
    n = len(terms)
    rows, code = to_next.shape
    own = pl.BlockSpec((rows, code), lambda i: (0, 0))
    return pl.pallas_call(
        functools.partial(ring_add_kernel, n),
        grid=(1,),
        out_shape=(shape((rows, code), BF16),) * 2,
        in_specs=[block_of(t, 8, LATE[0]) for t in terms]
        + [own]
        + [block_of(t, 8, LATE[1]) for t in terms]
        + [own],
        out_specs=(own,) * 2,
        compiler_params=params(),
        name="ring_add",
    )(*terms, to_next, *terms, to_prev)


def pair_sum_kernel(*refs):
    refs[-1][...] = sum_of(refs[:-1]).astype(BF16)


def pair_sum(terms, near):
    rows, code = near[0].shape
    own = pl.BlockSpec((rows, code), lambda i: (0, 0))
    return pl.pallas_call(
        pair_sum_kernel,
        grid=(1,),
        out_shape=shape((rows, code), BF16),
        in_specs=[block_of(t, 8, 1) for t in terms] + [own] * len(near),
        out_specs=own,
        compiler_params=params(),
        name="pair_sum",
    )(*terms, *near)


def final_kernel(*refs):
    codes, out = refs[-2:]
    total = sum_of(refs[:-2])
    values = codes[...].astype(F32)
    norm = norm_of(values)
    units = values / norm
    inner = jnp.sum(total * units, axis=1, keepdims=True)
    out[...] = ((total - units * inner) / norm).astype(BF16)


def finish(terms, near, got, codes):
    own = pl.BlockSpec(codes.shape, lambda i: (0, 0))
    return pl.pallas_call(
        final_kernel,
        grid=(1,),
        out_shape=shape(codes.shape, BF16),
        in_specs=[own] * (len(terms) + len(near) + 2),
        out_specs=own,
        compiler_params=params(),
        name="finish",
    )(*terms, *near, got, codes)


def fetch_images(where, images, held, sem, rows):
    copies = []
    for n, (k, j) in enumerate(PAIRS):
        start = pl.multiple_of(place(where, k, j) * rows, rows)
        copies.append(
            pltpu.make_async_copy(
                images[n].at[pl.ds(0, rows), :], held.at[pl.ds(start, rows), :], sem.at[n]
            )
        )
    return copies


def fetch_texts(texts, held, sem, rows, part):
    return [
        pltpu.make_async_copy(
            texts[n].at[pl.ds(part * rows, rows), :], held.at[pl.ds(n * rows, rows), :], sem.at[n]
        )
        for n in range(16)
    ]


def wait_texts(copies, step, columns, rows):
    done = 0
    for at in range(16 * rows // columns):
        need = min(16, -(-(at + 1) * columns // rows))

        @pl.when(step == at)
        def _():
            for copy in copies[done:need]:
                copy.wait()

        done = need


ROW_TILE = 256
COLS = 512


def lanes_of(value):
    return [value[:, n * LANES : (n + 1) * LANES] for n in range(value.shape[1] // LANES)]


def student_kernel(where, scale, *refs):
    images, texts = refs[:8], refs[8:24]
    slog, mout, sout = refs[24:27]
    held, text, sem_image, sem_text = refs[27:]
    step = pl.program_id(0)
    rows = held.shape[0] // 8

    text_copies = fetch_texts(texts, text, sem_text, rows, 0)

    @pl.when(step == 0)
    def _():
        image_copies = fetch_images(where, images, held, sem_image, rows)
        for copy in image_copies + text_copies:
            copy.start()
        for copy in image_copies:
            copy.wait()
        mout[...] = jnp.full(mout.shape, -1e30, F32)
        sout[...] = jnp.zeros(sout.shape, F32)

    wait_texts(text_copies, step, COLS, rows)
    factor = scale[0] * LOG2E
    cols = text[pl.ds(pl.multiple_of(step * COLS, COLS), COLS), :]

    for r in range(held.shape[0] // ROW_TILE):
        at = pl.ds(r * ROW_TILE, ROW_TILE)
        s = factor * lax.dot_general(
            held[at, :], cols, (((1,), (1,)), ((), ())), preferred_element_type=F32
        )
        slog[at, :] = s
        old = mout[at, :]
        parts = lanes_of(s)
        top = functools.reduce(jnp.maximum, parts, old)
        total = sout[at, :] * jnp.exp2(old - top)
        for part in parts:
            total += jnp.exp2(part - top)
        mout[at, :] = top
        sout[at, :] = total


def student_logits(where, scale, images, texts):
    rows = images[0].shape[0] // 2 * 8
    code = images[0].shape[1]
    width = 8 * texts[0].shape[0]
    return pl.pallas_call(
        student_kernel,
        grid=(width // COLS,),
        out_shape=(
            shape((rows, width), F32),
            shape((rows, LANES), F32),
            shape((rows, LANES), F32),
        ),
        in_specs=[SMEM, SMEM] + [ANY] * 24,
        out_specs=(
            pl.BlockSpec((rows, COLS), lambda i: (0, i)),
            pl.BlockSpec((rows, LANES), lambda i: (0, 0)),
            pl.BlockSpec((rows, LANES), lambda i: (0, 0)),
        ),
        scratch_shapes=[
            pltpu.VMEM((rows, code), BF16),
            pltpu.VMEM((width, code), BF16),
            pltpu.SemaphoreType.DMA((8,)),
            pltpu.SemaphoreType.DMA((16,)),
        ],
        compiler_params=params(),
        cost_estimate=pl.CostEstimate(
            flops=2 * rows * width * code, bytes_accessed=4 * rows * width, transcendentals=0
        ),
        name="student_logits",
    )(where, scale, *images, *texts)


def teacher_images_kernel(*refs):
    images, held, raw, sem = refs[:8], *refs[8:]
    rows = raw.shape[1]
    copies = [
        pltpu.make_async_copy(images[n].at[pl.ds(rows, rows), :], raw.at[n], sem.at[n])
        for n in range(8)
    ]
    for copy in copies:
        copy.start()
    for copy in copies:
        copy.wait()

    def block(l, carry):
        at = pl.ds(pl.multiple_of(l * LANES, LANES), LANES)
        values = [raw[n, :, at].astype(F32) for n in range(8)]
        square = sum(v * v for v in values)
        norm = jnp.sqrt(jnp.sum(square, axis=1, keepdims=True) + EPS)
        to = pl.ds(pl.multiple_of(l * rows, rows), rows)
        for n in range(8):
            held[to, n * LANES : (n + 1) * LANES] = (values[n] / norm).astype(BF16)
        return carry

    lax.fori_loop(0, 8, block, 0)


def teacher_images(images):
    rows, code = images[0].shape
    return pl.pallas_call(
        teacher_images_kernel,
        out_shape=shape((4 * rows, code), BF16),
        in_specs=[ANY] * 8,
        out_specs=VMEM,
        scratch_shapes=[pltpu.VMEM((8, rows // 2, code), BF16), pltpu.SemaphoreType.DMA((8,))],
        compiler_params=params(),
        name="teacher_images",
    )(*images)


def teacher_kernel(scale, *refs):
    held, texts = refs[0], refs[1:17]
    slog, ms, ss = refs[17:20]
    tlog, stats = refs[20:22]
    text, mt, st, ct, sem_text = refs[22:]
    step = pl.program_id(0)
    rows = held.shape[0] // 8
    text_copies = fetch_texts(texts, text, sem_text, rows, 1)

    @pl.when(step == 0)
    def _():
        for copy in text_copies:
            copy.start()
        mt[...] = jnp.full(mt.shape, -1e30, F32)
        st[...] = jnp.zeros(st.shape, F32)
        ct[...] = jnp.zeros(ct.shape, F32)

    wait_texts(text_copies, step, COLS, rows)
    factor = scale[0] * LOG2E
    cols = text[pl.ds(pl.multiple_of(step * COLS, COLS), COLS), :]

    for r in range(held.shape[0] // ROW_TILE):
        at = pl.ds(r * ROW_TILE, ROW_TILE)
        t = factor * lax.dot_general(
            held[at, :], cols, (((1,), (1,)), ((), ())), preferred_element_type=F32
        )
        tlog[at, :] = t
        s_parts = lanes_of(slog[at, :])
        t_parts = lanes_of(t)
        old = mt[at, :]
        top = functools.reduce(jnp.maximum, t_parts, old)
        shrink = jnp.exp2(old - top)
        total = st[at, :] * shrink
        cross = ct[at, :] * shrink
        for a, b in zip(t_parts, s_parts):
            e = jnp.exp2(a - top)
            total += e
            cross += e * (a - b)
        mt[at, :] = top
        st[at, :] = total
        ct[at, :] = cross

    @pl.when(step == pl.num_programs(0) - 1)
    def _():
        smax = jnp.max(ms[...], axis=1, keepdims=True)
        ssum = jnp.sum(ss[...] * jnp.exp2(ms[...] - smax), axis=1, keepdims=True)
        tmax = jnp.max(mt[...], axis=1, keepdims=True)
        shrink = jnp.exp2(mt[...] - tmax)
        tsum = jnp.sum(st[...] * shrink, axis=1, keepdims=True)
        cross = jnp.sum(ct[...] * shrink, axis=1, keepdims=True)
        lane = lax.broadcasted_iota(jnp.int32, ms.shape, 1)
        packed = jnp.zeros(ms.shape, F32)
        values = (smax + jnp.log2(ssum), tmax + jnp.log2(tsum), cross / tsum)
        for n, value in enumerate(values):
            packed = jnp.where(lane == n, value, packed)
        turned = packed.T[:8, :]
        count = turned.shape[1] // LANES
        lines = [turned[n : n + 1, c * LANES : (c + 1) * LANES] for n in range(3) for c in range(count)]
        lines.append(jnp.zeros((stats.shape[1] - 3 * count, LANES), F32))
        block = jnp.concatenate(lines, axis=0)
        for n in range(8):
            stats[n] = block


def teacher_logits(scale, image, texts, slog, ms, ss):
    rows, width = slog.shape
    code = image.shape[1]
    lines = -(-(3 * rows // LANES + 1) // 8) * 8
    whole = pl.BlockSpec((rows, LANES), lambda i: (0, 0))
    return pl.pallas_call(
        teacher_kernel,
        grid=(width // COLS,),
        out_shape=(shape((rows, width), F32), shape((8, lines, LANES), F32)),
        in_specs=[SMEM, pl.BlockSpec((rows, code), lambda i: (0, 0))]
        + [ANY] * 16
        + [pl.BlockSpec((rows, COLS), lambda i: (0, i)), whole, whole],
        out_specs=(
            pl.BlockSpec((rows, COLS), lambda i: (0, i)),
            pl.BlockSpec((8, lines, LANES), lambda i: (0, 0, 0)),
        ),
        scratch_shapes=[
            pltpu.VMEM((width, code), BF16),
            pltpu.VMEM((rows, LANES), F32),
            pltpu.VMEM((rows, LANES), F32),
            pltpu.VMEM((rows, LANES), F32),
            pltpu.SemaphoreType.DMA((16,)),
        ],
        compiler_params=params(),
        cost_estimate=pl.CostEstimate(
            flops=2 * rows * width * code, bytes_accessed=8 * rows * width, transcendentals=0
        ),
        name="teacher_logits",
    )(scale, image, *texts, slog, ms, ss)


def merge_stats(stats, lses, lset, loss):
    rows = lses.shape[0]
    count = rows // LANES
    part_s, part_t, ratio = [
        jnp.concatenate([stats[:, n * count + c, :] for c in range(count)], axis=1) for n in range(3)
    ]
    smax = jnp.max(part_s, axis=0, keepdims=True)
    lse_s = smax + jnp.log2(jnp.sum(jnp.exp2(part_s - smax), axis=0, keepdims=True))
    tmax = jnp.max(part_t, axis=0, keepdims=True)
    weight = jnp.exp2(part_t - tmax)
    tsum = jnp.sum(weight, axis=0, keepdims=True)
    cross = jnp.sum(ratio * weight, axis=0, keepdims=True)
    lse_t = tmax + jnp.log2(tsum)
    diverge = LN2 * (cross / tsum - lse_t + lse_s)
    loss[...] = jnp.full(loss.shape, jnp.sum(diverge), F32)
    lses[...] = jnp.broadcast_to(lse_s, (LANES, rows)).T
    lset[...] = jnp.broadcast_to(lse_t, (LANES, rows)).T


GCOLS = 256


def grads_kernel(where, scale, *refs):
    images, texts = refs[:8], refs[8:24]
    slog, tlog, stats = refs[24:27]
    keep, away, dimg, *early, loss = refs[27:35]
    held, text, grad, acc, low, lses, lset, sem_image, sem_text, sem_out = refs[35:]
    step = pl.program_id(0)
    steps = pl.num_programs(0)
    rows = held.shape[0] // 8
    image_copies = fetch_images(where, images, held, sem_image, rows)
    text_copies = fetch_texts(texts, text, sem_text, rows, 0)

    @pl.when(step == 0)
    def _():
        for copy in text_copies[:2] + image_copies + text_copies[2:]:
            copy.start()
        acc[...] = jnp.zeros(acc.shape, F32)
        merge_stats(stats, lses, lset, loss)
        for copy in image_copies:
            copy.wait()

    wait_texts(text_copies, step, GCOLS, rows)
    cols = text[pl.ds(pl.multiple_of(step * GCOLS, GCOLS), GCOLS), :]

    for r in range(held.shape[0] // ROW_TILE):
        at = pl.ds(r * ROW_TILE, ROW_TILE)
        ls, lt = lses[at, :], lset[at, :]
        parts = []
        for a, b in zip(lanes_of(slog[at, :]), lanes_of(tlog[at, :])):
            parts.append((scale[0] * (jnp.exp2(a - ls) - jnp.exp2(b - lt))).astype(BF16))
        g = jnp.concatenate(parts, axis=1)
        grad[at, :] = g
        acc[at, :] += jnp.dot(g, cols, preferred_element_type=F32)

    term = lax.dot_general(
        grad[...], held[...], (((0,), (0,)), ((), ())), preferred_element_type=F32
    ).astype(BF16)

    @pl.when(step < steps // 2)
    def _():
        keep[...] = term

    @pl.when(step >= steps // 2)
    def _():
        away[...] = term

    @pl.when(step == steps - 1)
    def _():
        low[...] = acc[...].astype(BF16)
        copies = []
        for n, (k, j) in enumerate(PAIRS):
            start = pl.multiple_of(place(where, k, j) * rows, rows)
            target = dimg.at[pl.ds(n * rows, rows), :]
            if n in EARLY:
                target = early[EARLY.index(n)]
            copies.append(
                pltpu.make_async_copy(low.at[pl.ds(start, rows), :], target, sem_out.at[n])
            )
        for copy in copies:
            copy.start()
        for copy in copies:
            copy.wait()


def grads(where, scale, images, texts, slog, tlog, stats):
    rows, width = slog.shape
    code = images[0].shape[1]
    own = rows // 8
    steps = width // GCOLS
    half = steps // 2
    column = pl.BlockSpec((rows, GCOLS), lambda i: (0, i))
    return pl.pallas_call(
        grads_kernel,
        grid=(steps,),
        out_shape=(
            shape((width // 2, code), BF16),
            shape((width // 2, code), BF16),
            shape((rows, code), BF16),
            *[shape((own, code), BF16)] * len(EARLY),
            shape((8, LANES), F32),
        ),
        in_specs=[SMEM, SMEM]
        + [ANY] * 24
        + [column, column, pl.BlockSpec(stats.shape, lambda i: (0, 0, 0))],
        out_specs=(
            pl.BlockSpec((GCOLS, code), lambda i: (jnp.minimum(i, half - 1), 0)),
            pl.BlockSpec((GCOLS, code), lambda i: (jnp.maximum(i - half, 0), 0)),
            *[ANY] * (1 + len(EARLY)),
            pl.BlockSpec((8, LANES), lambda i: (0, 0)),
        ),
        scratch_shapes=[
            pltpu.VMEM((rows, code), BF16),
            pltpu.VMEM((width, code), BF16),
            pltpu.VMEM((rows, GCOLS), BF16),
            pltpu.VMEM((rows, code), F32),
            pltpu.VMEM((rows, code), BF16),
            pltpu.VMEM((rows, LANES), F32),
            pltpu.VMEM((rows, LANES), F32),
            pltpu.SemaphoreType.DMA((8,)),
            pltpu.SemaphoreType.DMA((16,)),
            pltpu.SemaphoreType.DMA((8,)),
        ],
        compiler_params=params(),
        cost_estimate=pl.CostEstimate(
            flops=4 * rows * width * code, bytes_accessed=8 * rows * width, transcendentals=0
        ),
        name="grads",
    )(where, scale, *images, *texts, slog, tlog, stats)


def on_device(
    student_image, student_text, teacher_image, teacher_text, student_scale, teacher_scale
):
    rows = student_image.shape[0]
    loop = lax.axis_index("loop")
    where = jnp.stack([loop // 2, loop % 2]).astype(jnp.int32)

    parts = lax.all_to_all(
        teacher_text.reshape(8, rows, -1), "loop", split_axis=0, concat_axis=0
    )
    image_own = tie(own_image(student_image, teacher_image), parts)
    x_first = ring_own(image_own, "x", "yl")
    text_own = own_text(where, student_text, parts)
    z_first = ring_own(text_own, "z", "yh")
    x_second = ring_other(tie(x_first[2], x_first), "x")
    z_second = ring_other(tie(z_first[2], (x_first, z_first)), "z")
    x_third = ring_far(*tie((x_first[0], x_second[1]), (x_second, z_first)), "x")
    z_third = ring_far(*tie((z_first[0], z_second[1]), (x_second, z_second)), "z")
    images = in_order(image_own, x_first, x_second, x_third)
    timg = teacher_images(images)
    mine = in_order(text_own, z_first, z_second, tie(z_third, timg))
    texts = mine + [send(v, core=1) for v in mine]

    slog, ms, ss = student_logits(where, student_scale, images, texts)
    tlog, stats = teacher_logits(teacher_scale, timg, texts, slog, ms, ss)
    stats = lax.all_to_all(stats, "loop", split_axis=0, concat_axis=0)
    keep, away, dimg, *early, total = grads(
        where, student_scale, images, texts, slog, tlog, stats
    )
    got = send(away, core=1)

    def scatter(terms, early, ring):
        two, two_other, one_pair, three_own = early
        to_next = send(two, **{ring: 1})
        to_prev = send(two_other, **{ring: -1})
        pair_near = [send(one_pair, **{ring: 1})]
        own_near = [send(three_own, **{ring: -1})]
        ahead, behind = ring_add(terms, to_next, to_prev)
        own_near.append(send(ahead, **{ring: 1}))
        pair_near.append(send(behind, **{ring: -1}))
        return own_near, pair_near

    terms = (keep, got)
    x_own, x_pair = scatter((dimg,), early, "x")
    z_own, z_pair = scatter(terms, early_sum(terms), "z")
    for axis in ("core", "yh"):
        total = total + swap_bit(total, axis, 1)
    x_pair = tie(x_pair, total)
    x_got = send(pair_sum((dimg,), x_pair), yl=1)
    z_got = send(pair_sum(terms, z_pair), yh=1)
    total = tie(total, (z_own, z_pair))
    for bit in (1, 2):
        total = total + swap_bit(total, "z", bit)
    loss = (total[0, 0] / (rows * 128)).reshape(1)
    z_got = tie(z_got, total)
    return (
        loss,
        finish((dimg,), x_own, x_got, student_image),
        finish(terms, z_own, z_got, student_text),
    )


def solution(mesh):
    return jax.shard_map(
        on_device,
        mesh=mesh,
        in_specs=(
            P(("row", "loop"), None),
            P(("row", "loop"), None),
            P("row", "loop"),
            P("row", "loop"),
            P(),
            P(),
        ),
        out_specs=(P(), P(("row", "loop"), None), P(("row", "loop"), None)),
        check_vma=False,
    )
```
